32 devices in a mesh: ens: 2 (over y), comp: 4 (over z), tile: 2 (over x), sub: 2 (over core).
Axes of the slice: x: 2, y: 2, z: 4, core: 2. Of those that a mesh axis runs over, the one named last changes fastest.
Arguments:
- spectrum: bfloat16 [4, 8, 1296, 256], P(('ens', 'tile'), ('comp', 'sub')), parts along dimension 0, may hold values from 0.03 to 15, as said below
- wind_speed: float32 [4, 8, 256], P(('ens', 'tile'), ('comp', 'sub')), parts along dimension 0, may hold values from 2 to 25
- wind_dir: float32 [4, 8, 256], P(('ens', 'tile'), ('comp', 'sub')), parts along dimension 0, may hold values from -3.140625 to 3.140625
- freq_kernel: float32 [36, 36], replicated, may hold values from -1 to 1
- dir_kernel: float32 [36, 36], replicated, may hold values from -1 to 1
- depth: float32 [32, 128], P('tile'), may hold values from 10 to 4000
- current: float32 [2, 32, 128], P(None, 'tile'), may hold values from -3 to 3
- land_mask: int32 [32, 128], P('tile'), may hold values from 0 to 1, as said below
- tile_owner: int32 [2, 32], P('tile'), may hold values from 0 to 7, as said below
Outputs:
- spectrum_out: bfloat16 [4, 8, 1296, 256], P(('ens', 'tile'), ('comp', 'sub')), parts along dimension 0
The draws below stay inside these ranges and needn't reach their ends.
There are 2 independent parts, one for each index of `ens`. The reference program is written for one: setup_inputs(seed, part) draws one part's arguments, and reference() takes and returns one part's arrays. A program takes and returns all parts, laid end to end along the dimension named above; an argument that names none is the same for every part. Nothing has to cross between parts.
Inputs may be any that keep to these rules, and one draw needn't show every extreme that they name: `spectrum`: Positive. `land_mask`: 1 marks sea, 0 land. In every strip the busiest owner holds exactly 256 sea cells. `tile_owner`: in every strip each owner number appears exactly 4 times.
All inputs are finite; a program needn't handle non-finite values.
Results may differ from the reference program's by a relative error of at most 0.0016.
The reference program's roundings to bfloat16 on the way (of `source`) count: a program that leaves them out, or rounds other values in their place, can miss the bound.
Values may be sent and summed in bfloat16 or wider, within the bound.
A program may use at most 64 MiB of HBM per device.

```python
import math
import jax
import jax.numpy as jnp
from jax import lax

NF = 36
ND = 36
TS = 8
TPO = 4
TX = 2
NSUB = 2
K = 1296
NOWN = 8
PCAP = 256
BX = 16
TPS = 32
NY = 128
NX = 32
N_TILE = 2


def strip_owners(key):
    strips = NX // (TX * TS)
    keys = jax.random.split(key, strips + 1)
    orders = jax.vmap(lambda each_key: jax.random.permutation(each_key, TPS))(keys[:strips])
    owners = (orders // TPO).astype(jnp.int32)
    busiest = jax.random.randint(keys[strips], (strips,), 0, NOWN).astype(jnp.int32)
    return (owners, busiest)


def draw_tile_owner(key, part):
    owners, busiest = strip_owners(key)
    return owners


def draw_land_mask(key, part):
    owners, busiest = strip_owners(key)
    key = jax.random.fold_in(key, 7)
    kind_key, level_key, cell_key = jax.random.split(key, 3)
    strips = NX // (TX * TS)
    kinds = jax.random.randint(kind_key, (strips, TPS, 1), 0, 20).astype(jnp.int32)
    levels = jax.random.randint(level_key, (strips, TPS, 1), 20, 90).astype(jnp.int32)
    cell_draws = jax.random.randint(cell_key, (strips, TPS, TS * TS), 0, 100).astype(jnp.int32)
    mixed = (cell_draws < levels).astype(jnp.int32)
    tile_cells = jnp.where(kinds < 5, 1, jnp.where(kinds < 12, 0, mixed))
    forced = (owners == busiest[:, None])[:, :, None]
    tile_cells = jnp.where(forced, 1, tile_cells).astype(jnp.int32)
    tiles_down = NY // TS
    arranged = tile_cells.reshape(strips, TX, tiles_down, TS, TS).transpose(0, 1, 3, 2, 4)
    return arranged.reshape(NX, NY)


def draw_spectrum(key, part):
    key = jax.random.fold_in(key, 3)
    point_key, comp_key, rough_key = jax.random.split(key, 3)
    strips = NX // (TX * TS)
    point_scale = jnp.exp(jax.random.uniform(point_key, (strips, NOWN, 1, PCAP), jnp.float32, math.log(0.3), math.log(3.0)))
    comp_scale = jnp.exp(jax.random.uniform(comp_key, (1, 1, K, 1), jnp.float32, math.log(0.3), math.log(3.0)))
    roughness = jax.random.uniform(rough_key, (strips, NOWN, K, PCAP), jnp.float32, 0.5, 1.5)
    return (point_scale * comp_scale * roughness).astype(jnp.bfloat16)


def level_of(own_key, shape, pieces, smallest, top_value):
    loudness, own = 1.0, jax.random.fold_in(own_key, 6)
    for axis_at, blocks in pieces:
        heights = jnp.exp(jax.random.uniform(jax.random.fold_in(own, axis_at), (blocks,), jnp.float32, smallest / len(pieces), top_value / len(pieces)))
        loudness = loudness * jnp.repeat(heights, shape[axis_at] // blocks).reshape([-1 if axis == axis_at else 1 for axis in range(len(shape))])
    return loudness


def normal_values(stream_key, dims, spread, most, shards=(), kind=jnp.bfloat16):
    values = spread * jax.random.normal(stream_key, dims, jnp.float32)
    if shards:
        values = values * level_of(stream_key, dims, shards, -0.22, 0.18)
    return jnp.clip(values, -most, most).astype(kind)


def setup_inputs(seed: int = 0, part: int = 0) -> dict:
    seeds = jax.random.split(jax.random.key(seed), 10)
    part_splits = jax.random.split(jax.random.fold_in(seeds[9], part), 10)
    return {
        "spectrum": draw_spectrum(jax.random.fold_in(jax.random.fold_in(seeds[9], part), 71), part),
        "wind_speed": jnp.clip(jnp.exp(math.log(25.0) - 2.5257286 * jax.random.uniform(part_splits[1], (N_TILE, NOWN, PCAP), jnp.float32) ** level_of(part_splits[1], (N_TILE, NOWN, PCAP), ((0, 2), (1, 8)), -0.2, 0.2)), 2.0, 25.0),
        "wind_dir": jnp.clip(jax.random.uniform(part_splits[2], (N_TILE, NOWN, PCAP), jnp.float32, -3.140625, 3.140625), -3.140625, 3.140625),
        "freq_kernel": normal_values(seeds[3], (NF, NF), NF ** -0.5, 1.0, (), jnp.float32),
        "dir_kernel": normal_values(seeds[4], (ND, ND), ND ** -0.5, 1.0, (), jnp.float32),
        "depth": jnp.clip(jnp.exp(math.log(4000.0) - 5.9914645 * jax.random.uniform(seeds[5], (NX, NY), jnp.float32) ** level_of(seeds[5], (NX, NY), ((0, 2),), -0.2, 0.2)), 10.0, 4000.0),
        "current": normal_values(seeds[6], (2, NX, NY), 0.5, 3.0, ((1, 2),), jnp.float32),
        "land_mask": draw_land_mask(jax.random.fold_in(seeds[9], 71), part),
        "tile_owner": draw_tile_owner(jax.random.fold_in(seeds[9], 71), part),
    }


GRAVITY = 9.81
FREQ_BASE = 0.035
FREQ_RATIO = 1.1
TIME_STEP = 450.0
CELL_SIZE = 27750.0
LAT_EDGE = 64.0 * math.pi / 180.0
WIND_RATE = 0.1
BREAK_RATE = 0.15
ENERGY_REF = 1.5
TRANSFER_RATE = 0.2
KH_LIMIT = 10.0

def frequencies(how_many):
    return FREQ_BASE * jnp.power(jnp.float32(FREQ_RATIO), jnp.arange(how_many).astype(jnp.float32))

def directions(how_many):
    return 2.0 * math.pi * (jnp.arange(how_many).astype(jnp.float32) + 0.5) / how_many

def row_metric(rows_total):
    latitude = LAT_EDGE * (2.0 * (jnp.arange(rows_total).astype(jnp.float32) + 0.5) / rows_total - 1.0)
    return jnp.cos(latitude)

def group_speed(frequency, sea_depth):
    angular = 2.0 * math.pi * frequency
    deep_number = angular * angular / GRAVITY
    wavenumber = deep_number / jnp.sqrt(jnp.tanh(deep_number * sea_depth))
    relative = jnp.minimum(wavenumber * sea_depth, KH_LIMIT)
    group_ratio = 0.5 + relative / jnp.sinh(2.0 * relative)
    return group_ratio * angular / wavenumber

def source_terms(spectrum_block, wind_speed, heading, freq_kernel, dir_kernel):
    freq_count = freq_kernel.shape[0]
    dir_count = dir_kernel.shape[0]
    points = spectrum_block.shape[1]
    energy = spectrum_block.astype(jnp.float32).reshape(freq_count, dir_count, points)
    frequency = frequencies(freq_count)
    angles = directions(dir_count)
    weighted = lax.optimization_barrier(jnp.sum(energy, axis=1)) * frequency[:, None]
    first_moment = lax.optimization_barrier(jnp.sum(weighted, axis=0))
    mean_energy = first_moment / (dir_count * jnp.sum(frequency))
    mean_freq = lax.optimization_barrier(jnp.sum(weighted * frequency[:, None], axis=0)) / first_moment
    phase_speed = GRAVITY / (2.0 * math.pi * frequency)
    forcing = wind_speed[None, None, :] / phase_speed[:, None, None] * jnp.cos(angles[None, :, None] - heading[None, None, :]) - 1.0
    growth = WIND_RATE * jnp.maximum(forcing, 0.0)
    damping = BREAK_RATE * (frequency[:, None, None] / mean_freq[None, None, :]) * jnp.square(mean_energy / ENERGY_REF)[None, None, :]
    coupled = jnp.einsum('ab,bjp->ajp', freq_kernel, energy, precision=lax.Precision.HIGHEST)
    coupled = jnp.einsum('cj,ajp->acp', dir_kernel, coupled, precision=lax.Precision.HIGHEST)
    transfer = TRANSFER_RATE * energy * coupled / mean_energy[None, None, :]
    updated = (energy + growth * energy + transfer) / (1.0 + damping)
    return updated.reshape(freq_count * dir_count, points).astype(jnp.bfloat16)

def window(values, begin_at, end_at, along):
    return lax.slice_in_dim(values, begin_at, end_at, axis=along)

def upwind_sweep(density, courant, sea_mask, along):
    length = density.shape[along]
    behind = window(density, 0, length - 3, along)
    centre = window(density, 1, length - 2, along)
    ahead_one = window(density, 2, length - 1, along)
    beyond = window(density, 3, length, along)
    face_courant = 0.5 * (window(courant, 1, length - 2, along) + window(courant, 2, length - 1, along))
    face_courant = face_courant * window(sea_mask, 1, length - 2, along) * window(sea_mask, 2, length - 1, along)
    curvature = (1.0 - face_courant * face_courant) / 6.0
    middle = 0.5 * (centre + ahead_one) - 0.5 * face_courant * (ahead_one - centre)
    upstream = jnp.where(face_courant > 0.0, ahead_one - 2.0 * centre + behind, beyond - 2.0 * ahead_one + centre)
    face_flux = face_courant * (middle - curvature * upstream)
    return window(density, 2, length - 2, along) - (window(face_flux, 1, length - 3, along) - window(face_flux, 0, length - 4, along))

def layout_maps(mask_strip, owners, owner_count):
    strip_width, strip_height = mask_strip.shape
    tiles_across = strip_width // TS
    tiles_down = strip_height // TS
    tile_cells = mask_strip.reshape(tiles_across, TS, tiles_down, TS).transpose(0, 2, 1, 3).reshape(tiles_across * tiles_down, TS * TS)
    counts = lax.optimization_barrier(jnp.sum(tile_cells, axis=1)).astype(jnp.int32)
    tile_index = jnp.arange(tiles_across * tiles_down).astype(jnp.int32)
    earlier = (owners[None, :] == owners[:, None]) & (tile_index[None, :] < tile_index[:, None])
    offsets = lax.optimization_barrier(jnp.sum(jnp.where(earlier, counts[None, :], 0), axis=1)).astype(jnp.int32)
    rank_within = (jnp.cumsum(tile_cells, axis=1) - tile_cells).astype(jnp.int32)
    columns = owners[:, None] * PCAP + offsets[:, None] + rank_within
    columns = columns.reshape(tiles_across, tiles_down, TS, TS).transpose(0, 2, 1, 3).reshape(strip_width * strip_height).astype(jnp.int32)
    sea_cells = mask_strip.reshape(strip_width * strip_height)
    targets = jnp.where(sea_cells == 1, columns, owner_count * PCAP).astype(jnp.int32)
    cell_numbers = jnp.arange(strip_width * strip_height).astype(jnp.int32)
    slot_cell = jnp.zeros((owner_count * PCAP,), jnp.int32).at[targets].set(cell_numbers, mode='drop')
    filled = jnp.zeros((owner_count * PCAP,), jnp.int32).at[targets].set(jnp.ones_like(cell_numbers), mode='drop')
    return (columns, sea_cells, slot_cell, filled)

def wrap_first(values):
    return jnp.pad(values, ((0, 0), (2, 2), (0, 0)), mode='wrap')

def close_second(values):
    return jnp.pad(values, ((0, 0), (0, 0), (2, 2)))

def reference(spectrum, wind_speed, wind_dir, freq_kernel, dir_kernel, depth, current, land_mask, tile_owner):
    strips = spectrum.shape[0]
    owner_count = spectrum.shape[1]
    flat_source = lax.map(lambda items: source_terms(items[0], items[1], items[2], freq_kernel, dir_kernel), (spectrum.reshape(strips * owner_count, K, PCAP), wind_speed.reshape(strips * owner_count, PCAP), wind_dir.reshape(strips * owner_count, PCAP)))
    source = flat_source.reshape(strips, owner_count, K, PCAP)
    column_list = []
    sea_list = []
    slot_list = []
    filled_list = []
    for strip_number in range(strips):
        maps = layout_maps(land_mask[strip_number * BX:(strip_number + 1) * BX], tile_owner[strip_number], owner_count)
        column_list.append(maps[0])
        sea_list.append(maps[1])
        slot_list.append(maps[2])
        filled_list.append(maps[3])
    columns = jnp.stack(column_list)
    sea_cells = jnp.stack(sea_list)
    slot_cell = jnp.stack(slot_list)
    filled = jnp.stack(filled_list)
    metric = row_metric(NY)
    angles = directions(ND)
    frequency_table = frequencies(NF)
    sea_full = land_mask.astype(jnp.float32)[None]

    def propagate(index):
        block = lax.dynamic_slice_in_dim(source, index * ND, ND, axis=2)
        gathered = block.transpose(0, 2, 1, 3).reshape(strips, ND, owner_count * PCAP)
        picked = jax.vmap(lambda table, where_from: jnp.take(table, where_from, axis=1, mode='clip'))(gathered, columns)
        density = jnp.where(sea_cells[:, None, :] == 1, picked.astype(jnp.float32), 0.0)
        density = density.reshape(strips, ND, BX, NY).transpose(1, 0, 2, 3).reshape(ND, NX, NY)
        group_vel = group_speed(frequency_table[index], depth)
        along_x = (group_vel[None] * jnp.cos(angles)[:, None, None] + current[0][None]) * TIME_STEP / (CELL_SIZE * metric[None, None, :])
        along_y = (group_vel[None] * jnp.sin(angles)[:, None, None] + current[1][None]) * TIME_STEP / CELL_SIZE
        for substep in range(NSUB):
            density = upwind_sweep(wrap_first(density), wrap_first(along_x), wrap_first(sea_full), 1)
            density = upwind_sweep(close_second(density), close_second(along_y), close_second(sea_full), 2)
        leaving = density.astype(jnp.bfloat16).reshape(ND, strips, BX * NY).transpose(1, 0, 2)
        chosen = jax.vmap(lambda table, where_from: jnp.take(table, where_from, axis=1, mode='clip'))(leaving, slot_cell)
        chosen = jnp.where(filled[:, None, :] == 1, chosen, jnp.zeros((), jnp.bfloat16))
        return chosen.reshape(strips, ND, owner_count, PCAP).transpose(0, 2, 1, 3)
    stacked = lax.map(propagate, jnp.arange(NF).astype(jnp.int32))
    return stacked.transpose(1, 2, 0, 3, 4).reshape(strips, owner_count, K, PCAP)
```

```python
import math

import jax
import jax.numpy as jnp
from jax import lax
from jax.experimental import pallas as pl
from jax.experimental.pallas import tpu as pltpu
from jax.sharding import PartitionSpec as P

NF = 36
ND = 36
TS = 8
NSUB = 2
K = 1296
PCAP = 256


GRAVITY = 9.81
FREQ_BASE = 0.035
FREQ_RATIO = 1.1
TIME_STEP = 450.0
CELL_SIZE = 27750.0
LAT_EDGE = 64.0 * math.pi / 180.0
WIND_RATE = 0.1
BREAK_RATE = 0.15
ENERGY_REF = 1.5
TRANSFER_RATE = 0.2
KH_LIMIT = 10.0


def padded(value, sides, width):
    for axis, dim in sides:
        devices, length = (lax.axis_size(axis), value.shape[dim])
        up = [(i, (i + 1) % devices) for i in range(devices)]
        down = [(j, i) for i, j in up]
        last = lax.slice_in_dim(value, length - width, length, axis=dim)
        leading = lax.slice_in_dim(value, 0, width, axis=dim)
        before = lax.ppermute(last, axis, up)
        after = lax.ppermute(leading, axis, down)
        value = jnp.concatenate([before, value, after], axis=dim)
    return value


def frequencies(how_many):
    return FREQ_BASE * jnp.power(jnp.float32(FREQ_RATIO), jnp.arange(how_many).astype(jnp.float32))


def directions(how_many):
    return 2.0 * math.pi * (jnp.arange(how_many).astype(jnp.float32) + 0.5) / how_many


def row_metric(rows_total):
    latitude = LAT_EDGE * (
        2.0 * (jnp.arange(rows_total).astype(jnp.float32) + 0.5) / rows_total - 1.0
    )
    return jnp.cos(latitude)


def group_speed(frequency, sea_depth):
    angular = 2.0 * math.pi * frequency
    deep_number = angular * angular / GRAVITY
    wavenumber = deep_number / jnp.sqrt(jnp.tanh(deep_number * sea_depth))
    relative = jnp.minimum(wavenumber * sea_depth, KH_LIMIT)
    group_ratio = 0.5 + relative / jnp.sinh(2.0 * relative)
    return group_ratio * angular / wavenumber


def source_terms(spectrum_block, wind_speed, heading, freq_kernel, dir_kernel):
    freq_count = freq_kernel.shape[0]
    dir_count = dir_kernel.shape[0]
    points = spectrum_block.shape[1]
    energy = spectrum_block.astype(jnp.float32).reshape(freq_count, dir_count, points)
    frequency = frequencies(freq_count)
    angles = directions(dir_count)
    weighted = jnp.sum(energy, axis=1) * frequency[:, None]
    first_moment = jnp.sum(weighted, axis=0)
    mean_energy = first_moment / (dir_count * jnp.sum(frequency))
    mean_freq = jnp.sum(weighted * frequency[:, None], axis=0) / first_moment
    phase_speed = GRAVITY / (2.0 * math.pi * frequency)
    forcing = (
        wind_speed[None, None, :]
        / phase_speed[:, None, None]
        * jnp.cos(angles[None, :, None] - heading[None, None, :])
        - 1.0
    )
    growth = WIND_RATE * jnp.maximum(forcing, 0.0)
    damping = (
        BREAK_RATE
        * (frequency[:, None, None] / mean_freq[None, None, :])
        * jnp.square(mean_energy / ENERGY_REF)[None, None, :]
    )
    coupled = jnp.einsum("ab,bjp->ajp", freq_kernel, energy, precision=lax.Precision.HIGHEST)
    coupled = jnp.einsum("cj,ajp->acp", dir_kernel, coupled, precision=lax.Precision.HIGHEST)
    transfer = TRANSFER_RATE * energy * coupled / mean_energy[None, None, :]
    updated = (energy + growth * energy + transfer) / (1.0 + damping)
    return updated.reshape(freq_count * dir_count, points).astype(jnp.bfloat16)


def window(values, begin_at, end_at, along):
    return lax.slice_in_dim(values, begin_at, end_at, axis=along)


def upwind_sweep(density, courant, sea_mask, along):
    length = density.shape[along]
    behind = window(density, 0, length - 3, along)
    centre = window(density, 1, length - 2, along)
    ahead_one = window(density, 2, length - 1, along)
    beyond = window(density, 3, length, along)
    face_courant = 0.5 * (
        window(courant, 1, length - 2, along) + window(courant, 2, length - 1, along)
    )
    face_courant = (
        face_courant
        * window(sea_mask, 1, length - 2, along)
        * window(sea_mask, 2, length - 1, along)
    )
    curvature = (1.0 - face_courant * face_courant) / 6.0
    middle = 0.5 * (centre + ahead_one) - 0.5 * face_courant * (ahead_one - centre)
    upstream = jnp.where(
        face_courant > 0.0, ahead_one - 2.0 * centre + behind, beyond - 2.0 * ahead_one + centre
    )
    face_flux = face_courant * (middle - curvature * upstream)
    return window(density, 2, length - 2, along) - (
        window(face_flux, 1, length - 3, along) - window(face_flux, 0, length - 4, along)
    )


def column_sweep(density, courant, sea_mask):
    widths = ((0, 0), (0, 0), (2, 2))
    return upwind_sweep(
        jnp.pad(density, widths), jnp.pad(courant, widths), jnp.pad(sea_mask, widths), 2
    )


def layout_maps(mask_strip, owners, owner_count):
    strip_width, strip_height = mask_strip.shape
    tiles_across = strip_width // TS
    tiles_down = strip_height // TS
    tile_cells = (
        mask_strip.reshape(tiles_across, TS, tiles_down, TS)
        .transpose(0, 2, 1, 3)
        .reshape(tiles_across * tiles_down, TS * TS)
    )
    counts = jnp.sum(tile_cells, axis=1)
    tile_index = jnp.arange(tiles_across * tiles_down)
    earlier = (owners[None, :] == owners[:, None]) & (tile_index[None, :] < tile_index[:, None])
    offsets = jnp.sum(jnp.where(earlier, counts[None, :], 0), axis=1)
    rank_within = jnp.cumsum(tile_cells, axis=1) - tile_cells
    columns = owners[:, None] * PCAP + offsets[:, None] + rank_within
    columns = (
        columns.reshape(tiles_across, tiles_down, TS, TS)
        .transpose(0, 2, 1, 3)
        .reshape(strip_width * strip_height)
    )
    sea_cells = mask_strip.reshape(strip_width * strip_height)
    targets = jnp.where(sea_cells == 1, columns, owner_count * PCAP)
    cell_numbers = jnp.arange(strip_width * strip_height)
    slot_cell = (
        jnp.zeros((owner_count * PCAP,), jnp.int32).at[targets].set(cell_numbers, mode="drop")
    )
    filled = (
        jnp.zeros((owner_count * PCAP,), jnp.int32)
        .at[targets]
        .set(jnp.ones_like(cell_numbers), mode="drop")
    )
    return (columns, sea_cells, slot_cell, filled)


def local(
    spectrum, wind_speed, wind_dir, freq_kernel, dir_kernel, depth, current, land_mask, tile_owner
):
    owner_count = lax.axis_size("comp") * lax.axis_size("sub")
    group_size = -(-K // owner_count)
    padded_count = group_size * owner_count
    strip_width, strip_height = land_mask.shape
    columns, sea_cells, slot_cell, filled = layout_maps(land_mask, tile_owner[0], owner_count)
    rim_width = 2
    cell_stack = jnp.stack([depth, current[0], current[1], land_mask.astype(jnp.float32)])
    fields = padded(cell_stack.astype(jnp.bfloat16), (("tile", 1),), rim_width).astype(
        cell_stack.dtype
    )
    source = source_terms(spectrum[0, 0], wind_speed[0, 0], wind_dir[0, 0], freq_kernel, dir_kernel)
    outgoing = jnp.pad(source, ((0, padded_count - K), (0, 0)))
    arrived = lax.all_to_all(outgoing, ("comp", "sub"), split_axis=0, concat_axis=1, tiled=True)
    gathered = jnp.take(arrived, columns, axis=1, mode="clip")
    density = jnp.where(sea_cells[None, :] == 1, gathered.astype(jnp.float32), 0.0).reshape(
        group_size, strip_width, strip_height
    )
    group_index = lax.axis_index("comp") * lax.axis_size("sub") + lax.axis_index("sub")
    component = group_index * group_size + jnp.arange(group_size)
    frequency = frequencies(NF)[jnp.minimum(component // ND, NF - 1)]
    comp_angle = directions(ND)[component % ND]
    metric = row_metric(strip_height)
    group_vel = group_speed(frequency[:, None, None], fields[0][None])
    along_x = (
        (group_vel * jnp.cos(comp_angle)[:, None, None] + fields[1][None])
        * TIME_STEP
        / (CELL_SIZE * metric[None, None, :])
    )
    along_y = (
        (group_vel * jnp.sin(comp_angle)[:, None, None] + fields[2][None]) * TIME_STEP / CELL_SIZE
    )
    sea_field = fields[3][None]
    total_width = strip_width + 2 * rim_width
    inner_y = window(along_y, 2, total_width - 2, 1)
    inner_sea = window(sea_field, 2, total_width - 2, 1)
    for substep in range(NSUB):
        extended = padded(density, (("tile", 1),), 2)
        density = upwind_sweep(extended, along_x, sea_field, 1)
        density = column_sweep(density, inner_y, inner_sea)
    leaving = density.astype(jnp.bfloat16).reshape(group_size, strip_width * strip_height)
    picked = jnp.take(leaving, slot_cell, axis=1, mode="clip")
    picked = jnp.where(filled[None, :] == 1, picked, jnp.zeros((), jnp.bfloat16))
    returned = lax.all_to_all(picked, ("comp", "sub"), split_axis=1, concat_axis=0, tiled=True)
    return returned[:K].reshape(1, 1, K, PCAP)


OWNERS = 8
STRIPS = 2
GROUP = OWNERS * STRIPS
RANKS = 4
ROWS = 80
EXTRA = 16
CAP = ROWS + EXTRA
LAST = GROUP - 1
PARTS = ((0, 48), (48, 32))
PART_ROWS = 48
WIDE = 32
TALL = 128
FIELD_ROWS = 72


def butterfly(values, pieces):
    for bit in range(3):
        step = 1 << bit
        odd = (pieces & step) != 0
        values = [jnp.where(odd, values[(j + step) % 8], values[j]) for j in range(8)]
    return values


def turn(values, by):
    by %= values.shape[0]
    if by == 0:
        return values
    return jnp.concatenate([values[-by:], values[:-by]], axis=0)


def first_sweep(d, face, bend):
    ahead = turn(d, -1)
    slope = ahead - d
    second = slope - turn(slope, 1)
    upstream = jnp.where(face > 0.0, second, turn(second, -1))
    flux = face * (0.5 * (d + ahead) - 0.5 * face * slope - bend * upstream)
    return d - (flux - turn(flux, 1))


def second_sweep(d, face, bend, lane):
    shape = d.shape
    flat = lambda v: v.reshape(shape[0] * shape[1], shape[2])
    d, face, bend = flat(d), flat(face), flat(bend)
    ahead = jnp.where(lane == TALL - 1, 0.0, pltpu.roll(d, TALL - 1, 1))
    slope = ahead - d
    second = slope - jnp.where(lane == 0, d, pltpu.roll(slope, 1, 1))
    upstream = jnp.where(face > 0.0, second, pltpu.roll(second, TALL - 1, 1))
    flux = face * (0.5 * (d + ahead) - 0.5 * face * slope - bend * upstream)
    return (d - (flux - pltpu.roll(flux, 1, 1))).reshape(shape)


def exchange_kernel(
    source_ref, place_ref, field_ref, small_ref, angle_ref, out_ref,
    packed, arrived, fields, density, leaving, first_rate, second_rate, drift, tile_map,
    go_send, go_recv, go_extra_send, go_extra_recv,
    back_send, back_recv, back_extra_send, back_extra_recv, field_send, field_recv,
):
    comp, tile, sub = lax.axis_index("comp"), lax.axis_index("tile"), lax.axis_index("sub")
    me = tile * OWNERS + comp * 2 + sub

    def partner(dc, dt, ds):
        c, t, s = lax.rem(comp + dc, 4), lax.rem(tile + dt, 2), lax.rem(sub + ds, 2)
        return t * OWNERS + c * 2 + s, {"comp": c, "tile": t, "sub": s}

    turns = [(dc, dt, ds) for dc in (2, 1, 3, 0) for dt in (0, 1) for ds in (0, 1)]
    turns = [item for item in turns if item != (0, 0, 0)]
    partners = [partner(*item) for item in turns]
    final_device = {"comp": 3, "tile": 1, "sub": 1}

    barrier = pltpu.get_barrier_semaphore()
    for _, where in partners:
        pl.semaphore_signal(barrier, inc=1, device_id=where, device_id_type=pl.DeviceIdType.MESH)
    pl.semaphore_wait(barrier, GROUP - 1)

    def remote(src, dst, send, recv, where):
        return pltpu.make_async_remote_copy(
            src_ref=src, dst_ref=dst, send_sem=send, recv_sem=recv,
            device_id=where, device_id_type=pl.DeviceIdType.MESH,
        )

    beside = partner(0, 1, 0)[1]
    field_copy = remote(field_ref, fields.at[tile], field_send, field_recv, beside)
    field_copy.start()

    packed[...] = jnp.dot(
        source_ref[...], place_ref[...], preferred_element_type=jnp.float32
    ).astype(jnp.bfloat16)

    def aligned(value):
        return pl.multiple_of(value, 16)

    def go(part, number, where):
        at, rows = PARTS[part]
        return remote(
            packed.at[pl.ds(aligned(number * ROWS + at), rows)],
            arrived.at[me, pl.ds(at, rows)],
            go_send.at[part, number], go_recv.at[part, me], where,
        )

    def go_landed(part, number, where):
        at, rows = PARTS[part]
        spot = arrived.at[number, pl.ds(at, rows)]
        return remote(spot, spot, go_send.at[part, number], go_recv.at[part, number], where)

    def go_extra():
        return remote(
            packed.at[pl.ds(GROUP * ROWS, EXTRA)], arrived.at[me, pl.ds(ROWS, EXTRA)],
            go_extra_send, go_extra_recv.at[me], final_device,
        )

    for part in range(len(PARTS)):
        for number, where in partners:
            go(part, number, where).start()

    @pl.when(me != LAST)
    def _():
        go_extra().start()

    arrived[me, pl.ds(0, ROWS)] = packed[pl.ds(aligned(me * ROWS), ROWS), :]

    @pl.when(me == LAST)
    def _():
        arrived[LAST, pl.ds(ROWS, EXTRA)] = packed[pl.ds(GROUP * ROWS, EXTRA), :]

    @pl.when(me != LAST)
    def _():
        for number in range(GROUP):
            arrived[number, pl.ds(ROWS, EXTRA)] = jnp.zeros((EXTRA, 256), jnp.bfloat16)

    fields[tile] = field_ref[...]
    field_copy.wait()

    lane = lax.broadcasted_iota(jnp.int32, (1, TALL), 1)
    row_number = lax.broadcasted_iota(jnp.int32, (256, TALL), 0)
    for strip in range(STRIPS):
        for half in range(2):
            target = fields[strip, pl.ds(64 + half, 1), :].astype(jnp.int32)
            tile_map[strip, :, pl.ds(half * TALL, TALL)] = jnp.where(
                row_number == target, 1.0, 0.0
            ).astype(jnp.bfloat16)

    def whole(at):
        return jnp.concatenate([fields[strip, pl.ds(at, 16), :] for strip in range(STRIPS)], axis=0)

    depth, along_u, along_v, sea = whole(0), whole(16), whole(32), whole(48)
    above = lambda v: jnp.concatenate([v[1:], v[:1]], axis=0)
    beyond = lambda v: jnp.where(lane == TALL - 1, 0.0, pltpu.roll(v, TALL - 1, 1))
    step_x = small_ref[pl.ds(4, 1), :]
    half_x = 0.5 * step_x * sea * above(sea)
    half_y = 0.5 * (TIME_STEP / CELL_SIZE) * sea * beyond(sea)

    def spread(ref, at, value):
        for x in range(WIDE):
            ref[at, x] = jnp.broadcast_to(value[x : x + 1, :], (8, TALL))

    spread(drift, 0, half_x * (along_u + above(along_u)))
    spread(drift, 1, half_y * (along_v + beyond(along_v)))
    for which in range(4):
        frequency = small_ref[pl.ds(which, 1), :]
        angular = 2.0 * math.pi * frequency
        deep_number = angular * angular / GRAVITY
        wavenumber = deep_number / jnp.sqrt(jnp.tanh(deep_number * depth))
        relative = jnp.minimum(wavenumber * depth, KH_LIMIT)
        sinh = 0.5 * (jnp.exp(2.0 * relative) - jnp.exp(-2.0 * relative))
        speed = (0.5 + relative / sinh) * angular / wavenumber
        spread(first_rate, which, half_x * (speed + above(speed)))
        spread(second_rate, which, half_y * (speed + beyond(speed)))

    pieces = lax.shift_right_logical(lax.broadcasted_iota(jnp.int32, (1, 256), 1), 5)
    base = me * ROWS
    first_index = base // ND
    row8 = lax.broadcasted_iota(jnp.int32, (8, TALL), 0)
    wide_lane = lax.broadcasted_iota(jnp.int32, (WIDE * 8, TALL), 1)

    def back(part, number, where):
        at, rows = PARTS[part]
        return remote(
            leaving.at[number, pl.ds(at, rows)],
            out_ref.at[pl.ds(aligned(me * ROWS + at), rows)],
            back_send.at[part, number], back_recv.at[part, me], where,
        )

    def back_landed(part, number, where):
        at, rows = PARTS[part]
        spot = out_ref.at[pl.ds(aligned(number * ROWS + at), rows)]
        return remote(spot, spot, back_send.at[part, number], back_recv.at[part, number], where)

    def back_extra(number, where):
        return remote(
            leaving.at[number, pl.ds(ROWS, EXTRA)], out_ref.at[pl.ds(GROUP * ROWS, EXTRA)],
            back_extra_send.at[number], back_extra_recv, where,
        )

    for part in range(len(PARTS)):
        at, rows = PARTS[part]
        for number, where in partners:
            go_landed(part, number, where).wait_recv()
        if part == 1:

            @pl.when(me == LAST)
            def _():
                for number, where in partners:
                    spot = arrived.at[number, pl.ds(ROWS, EXTRA)]
                    remote(spot, spot, go_extra_send, go_extra_recv.at[number], where).wait_recv()

        for strip in range(STRIPS):
            blocks = [
                arrived[strip * OWNERS + o, pl.ds(at, PART_ROWS), :].astype(jnp.float32)
                for o in range(OWNERS)
            ]
            blocks = butterfly(blocks, pieces)
            lined = []
            for xx in range(TS):
                block = blocks[-xx % 8]
                if xx:
                    block = pltpu.roll(block, 256 - 32 * xx, 1)
                lined.append(block.astype(jnp.bfloat16))
            placed = jnp.dot(
                jnp.concatenate(lined, axis=0), tile_map[strip], preferred_element_type=jnp.float32
            )
            for xx in range(TS):
                for half in range(2):
                    density[strip * 16 + half * TS + xx] = placed[
                        xx * PART_ROWS : (xx + 1) * PART_ROWS, half * TALL : (half + 1) * TALL
                    ]

        def chunk(step, carry):
            start = base + at + step * 8
            index = start // ND
            table = index - first_index
            later = jnp.minimum(table + 1, 3)
            new = row8 >= (index + 1) * ND - start
            here = pl.ds(pl.multiple_of(step * 8, 8), 8)
            angle_at = pl.ds(pl.multiple_of(at + step * 8, 8), 8)
            cos, sin = angle_ref[0, angle_at, :], angle_ref[1, angle_at, :]
            face_x = jnp.where(new[None], first_rate[later], first_rate[table]) * cos[None] + drift[0]
            face_y = jnp.where(new[None], second_rate[later], second_rate[table]) * sin[None] + drift[1]
            bend_x = (1.0 - face_x * face_x) * (1.0 / 6.0)
            bend_y = (1.0 - face_y * face_y) * (1.0 / 6.0)
            d = density[:, here, :]
            for substep in range(NSUB):
                d = first_sweep(d, face_x, bend_x)
                d = second_sweep(d, face_y, bend_y, wide_lane)
            density[:, here, :] = d
            return carry

        count = PART_ROWS // 8 if part == 0 else jnp.where(me == LAST, PART_ROWS // 8, rows // 8)
        lax.fori_loop(0, count, chunk, 0)

        for strip in range(STRIPS):
            lined = [
                jnp.concatenate(
                    [density[strip * 16 + xx], density[strip * 16 + TS + xx]], axis=1
                ).astype(jnp.bfloat16)
                for xx in range(TS)
            ]
            sorted_rows = lax.dot_general(
                jnp.concatenate(lined, axis=0), tile_map[strip], (((1,), (1,)), ((), ())),
                preferred_element_type=jnp.float32,
            )
            blocks = []
            for xx in range(TS):
                block = sorted_rows[xx * PART_ROWS : (xx + 1) * PART_ROWS]
                blocks.append(pltpu.roll(block, 32 * xx, 1) if xx else block)
            blocks = butterfly(blocks, pieces)
            for o in range(OWNERS):
                leaving[strip * OWNERS + o, pl.ds(at, PART_ROWS)] = blocks[-o % 8].astype(jnp.bfloat16)

        for number, where in partners:
            back(part, number, where).start()
        if part == 1:

            @pl.when(me == LAST)
            def _():
                for number, where in partners:
                    back_extra(number, where).start()

    out_ref[pl.ds(aligned(me * ROWS), ROWS), :] = leaving[me, pl.ds(0, ROWS), :]

    @pl.when(me == LAST)
    def _():
        out_ref[pl.ds(GROUP * ROWS, EXTRA), :] = leaving[LAST, pl.ds(ROWS, EXTRA), :]

    for part in range(len(PARTS)):
        for number, where in partners:
            go(part, number, where).wait_send()
            back(part, number, where).wait_send()
            back_landed(part, number, where).wait_recv()

    @pl.when(me != LAST)
    def _():
        go_extra().wait_send()
        spot = out_ref.at[pl.ds(GROUP * ROWS, EXTRA)]
        remote(spot, spot, back_extra_send.at[LAST], back_extra_recv, final_device).wait_recv()

    @pl.when(me == LAST)
    def _():
        for number, where in partners:
            back_extra(number, where).wait_send()


def exchange(source, place, field, small, angle):
    dma = pltpu.SemaphoreType.DMA
    vmem = pl.BlockSpec(memory_space=pltpu.VMEM)
    return pl.pallas_call(
        exchange_kernel,
        out_shape=jax.ShapeDtypeStruct((K, 256), jnp.bfloat16),
        in_specs=[vmem] * 5,
        out_specs=vmem,
        scratch_shapes=[
            pltpu.VMEM((K, 256), jnp.bfloat16),
            pltpu.VMEM((GROUP, CAP, 256), jnp.bfloat16),
            pltpu.VMEM((STRIPS, FIELD_ROWS, TALL), jnp.float32),
            pltpu.VMEM((WIDE, PART_ROWS, TALL), jnp.float32),
            pltpu.VMEM((GROUP, CAP, 256), jnp.bfloat16),
            pltpu.VMEM((4, WIDE, 8, TALL), jnp.float32),
            pltpu.VMEM((4, WIDE, 8, TALL), jnp.float32),
            pltpu.VMEM((2, WIDE, 8, TALL), jnp.float32),
            pltpu.VMEM((STRIPS, 256, 256), jnp.bfloat16),
            dma((2, GROUP)), dma((2, GROUP)), dma, dma((GROUP,)),
            dma((2, GROUP)), dma((2, GROUP)), dma((GROUP,)), dma, dma, dma,
        ],
        compiler_params=pltpu.CompilerParams(
            collective_id=0, has_side_effects=True, vmem_limit_bytes=40 * 1024 * 1024
        ),
    )(source, place, field, small, angle)


def grouped(
    spectrum, wind_speed, wind_dir, freq_kernel, dir_kernel, depth, current, land_mask, tile_owner
):
    owner = lax.axis_index("comp") * lax.axis_size("sub") + lax.axis_index("sub")
    me = lax.axis_index("tile") * OWNERS + owner
    owners = tile_owner[0]
    tile_cells = (
        land_mask.reshape(2, TS, TALL // TS, TS).transpose(0, 2, 1, 3).reshape(32, 64)
    ).astype(jnp.float32)
    number = jnp.arange(32)
    same_before = (owners[None, :] == owners[:, None]) & (number[None, :] < number[:, None])
    rank = jnp.sum(same_before.astype(jnp.int32), axis=1)
    chosen = ((owners[None, :] == owner) & (rank[None, :] == jnp.arange(RANKS)[:, None])).astype(
        jnp.float32
    )
    mine = (chosen @ tile_cells).reshape(RANKS * 64)
    spot = jnp.arange(256)
    before = (spot[:, None] < spot[None, :]).astype(jnp.float32)
    slot = (mine[None, :] @ before)[0]
    slot = jnp.where(mine > 0.5, slot, -1.0)
    slot = slot.reshape(RANKS, TS, TS).transpose(1, 0, 2)
    slot = jnp.roll(slot, owner, axis=0).reshape(256)
    place = (slot[None, :] == spot.astype(jnp.float32)[:, None]).astype(jnp.bfloat16)
    target = (owners * 32 + rank * TS)[:, None] + jnp.arange(TS)[None, :]
    target = jnp.pad(target.reshape(2, TALL).astype(jnp.float32), ((0, 6), (0, 0)))
    field = jnp.concatenate(
        [depth, current[0], current[1], land_mask.astype(jnp.float32), target], axis=0
    )
    component = me * ROWS + jnp.arange(CAP)
    angles = directions(ND)[component % ND]
    angle = jnp.broadcast_to(
        jnp.stack([jnp.cos(angles), jnp.sin(angles)])[:, :, None], (2, CAP, TALL)
    )
    index = jnp.minimum((me * ROWS) // ND + jnp.arange(4), NF - 1)
    small = jnp.concatenate(
        [
            jnp.broadcast_to(frequencies(NF)[index][:, None], (4, TALL)),
            (TIME_STEP / (CELL_SIZE * row_metric(TALL)))[None],
            jnp.zeros((3, TALL), jnp.float32),
        ],
        axis=0,
    )
    source = source_terms(spectrum[0, 0], wind_speed[0, 0], wind_dir[0, 0], freq_kernel, dir_kernel)
    returned = exchange(source, place, field, small, angle)
    result = lax.dot_general(
        returned, place, (((1,), (1,)), ((), ())), preferred_element_type=jnp.float32
    ).astype(jnp.bfloat16)
    return result.reshape(1, 1, K, PCAP)


def solution(mesh):
    sizes = mesh.shape
    fits = (sizes["comp"], sizes["sub"], sizes["tile"]) == (4, 2, STRIPS)
    placed = (
        P(("ens", "tile"), ("comp", "sub"), None, None),
        P(("ens", "tile"), ("comp", "sub"), None),
        P(("ens", "tile"), ("comp", "sub"), None),
        P(),
        P(),
        P("tile", None),
        P(None, "tile", None),
        P("tile", None),
        P("tile", None),
    )
    return jax.shard_map(
        grouped if fits else local,
        mesh=mesh,
        in_specs=placed,
        out_specs=P(("ens", "tile"), ("comp", "sub"), None, None),
        check_vma=False,
    )
```

```python
import math

import jax
import jax.numpy as jnp
from jax import lax
from jax.experimental import pallas as pl
from jax.experimental.pallas import tpu as pltpu
from jax.sharding import PartitionSpec as P

NF = 36
ND = 36
TS = 8
NSUB = 2
K = 1296
PCAP = 256


GRAVITY = 9.81
FREQ_BASE = 0.035
FREQ_RATIO = 1.1
TIME_STEP = 450.0
CELL_SIZE = 27750.0
LAT_EDGE = 64.0 * math.pi / 180.0
WIND_RATE = 0.1
BREAK_RATE = 0.15
ENERGY_REF = 1.5
TRANSFER_RATE = 0.2
KH_LIMIT = 10.0


def padded(value, sides, width):
    for axis, dim in sides:
        devices, length = (lax.axis_size(axis), value.shape[dim])
        up = [(i, (i + 1) % devices) for i in range(devices)]
        down = [(j, i) for i, j in up]
        last = lax.slice_in_dim(value, length - width, length, axis=dim)
        leading = lax.slice_in_dim(value, 0, width, axis=dim)
        before = lax.ppermute(last, axis, up)
        after = lax.ppermute(leading, axis, down)
        value = jnp.concatenate([before, value, after], axis=dim)
    return value


def frequencies(how_many):
    return FREQ_BASE * jnp.power(jnp.float32(FREQ_RATIO), jnp.arange(how_many).astype(jnp.float32))


def directions(how_many):
    return 2.0 * math.pi * (jnp.arange(how_many).astype(jnp.float32) + 0.5) / how_many


def row_metric(rows_total):
    latitude = LAT_EDGE * (
        2.0 * (jnp.arange(rows_total).astype(jnp.float32) + 0.5) / rows_total - 1.0
    )
    return jnp.cos(latitude)


def group_speed(frequency, sea_depth):
    angular = 2.0 * math.pi * frequency
    deep_number = angular * angular / GRAVITY
    wavenumber = deep_number / jnp.sqrt(jnp.tanh(deep_number * sea_depth))
    relative = jnp.minimum(wavenumber * sea_depth, KH_LIMIT)
    group_ratio = 0.5 + relative / jnp.sinh(2.0 * relative)
    return group_ratio * angular / wavenumber


def source_terms(spectrum_block, wind_speed, heading, freq_kernel, dir_kernel):
    freq_count = freq_kernel.shape[0]
    dir_count = dir_kernel.shape[0]
    points = spectrum_block.shape[1]
    energy = spectrum_block.astype(jnp.float32).reshape(freq_count, dir_count, points)
    frequency = frequencies(freq_count)
    angles = directions(dir_count)
    weighted = jnp.sum(energy, axis=1) * frequency[:, None]
    first_moment = jnp.sum(weighted, axis=0)
    mean_energy = first_moment / (dir_count * jnp.sum(frequency))
    mean_freq = jnp.sum(weighted * frequency[:, None], axis=0) / first_moment
    phase_speed = GRAVITY / (2.0 * math.pi * frequency)
    forcing = (
        wind_speed[None, None, :]
        / phase_speed[:, None, None]
        * jnp.cos(angles[None, :, None] - heading[None, None, :])
        - 1.0
    )
    growth = WIND_RATE * jnp.maximum(forcing, 0.0)
    damping = (
        BREAK_RATE
        * (frequency[:, None, None] / mean_freq[None, None, :])
        * jnp.square(mean_energy / ENERGY_REF)[None, None, :]
    )
    coupled = jnp.einsum("ab,bjp->ajp", freq_kernel, energy, precision=lax.Precision.HIGH)
    coupled = jnp.einsum("cj,ajp->acp", dir_kernel, coupled, precision=lax.Precision.HIGH)
    transfer = TRANSFER_RATE * energy * coupled / mean_energy[None, None, :]
    updated = (energy + growth * energy + transfer) / (1.0 + damping)
    return updated.reshape(freq_count * dir_count, points).astype(jnp.bfloat16)


def window(values, begin_at, end_at, along):
    return lax.slice_in_dim(values, begin_at, end_at, axis=along)


def upwind_sweep(density, courant, sea_mask, along):
    length = density.shape[along]
    behind = window(density, 0, length - 3, along)
    centre = window(density, 1, length - 2, along)
    ahead_one = window(density, 2, length - 1, along)
    beyond = window(density, 3, length, along)
    face_courant = 0.5 * (
        window(courant, 1, length - 2, along) + window(courant, 2, length - 1, along)
    )
    face_courant = (
        face_courant
        * window(sea_mask, 1, length - 2, along)
        * window(sea_mask, 2, length - 1, along)
    )
    curvature = (1.0 - face_courant * face_courant) / 6.0
    middle = 0.5 * (centre + ahead_one) - 0.5 * face_courant * (ahead_one - centre)
    upstream = jnp.where(
        face_courant > 0.0, ahead_one - 2.0 * centre + behind, beyond - 2.0 * ahead_one + centre
    )
    face_flux = face_courant * (middle - curvature * upstream)
    return window(density, 2, length - 2, along) - (
        window(face_flux, 1, length - 3, along) - window(face_flux, 0, length - 4, along)
    )


def column_sweep(density, courant, sea_mask):
    widths = ((0, 0), (0, 0), (2, 2))
    return upwind_sweep(
        jnp.pad(density, widths), jnp.pad(courant, widths), jnp.pad(sea_mask, widths), 2
    )


def layout_maps(mask_strip, owners, owner_count):
    strip_width, strip_height = mask_strip.shape
    tiles_across = strip_width // TS
    tiles_down = strip_height // TS
    tile_cells = (
        mask_strip.reshape(tiles_across, TS, tiles_down, TS)
        .transpose(0, 2, 1, 3)
        .reshape(tiles_across * tiles_down, TS * TS)
    )
    counts = jnp.sum(tile_cells, axis=1)
    tile_index = jnp.arange(tiles_across * tiles_down)
    earlier = (owners[None, :] == owners[:, None]) & (tile_index[None, :] < tile_index[:, None])
    offsets = jnp.sum(jnp.where(earlier, counts[None, :], 0), axis=1)
    rank_within = jnp.cumsum(tile_cells, axis=1) - tile_cells
    columns = owners[:, None] * PCAP + offsets[:, None] + rank_within
    columns = (
        columns.reshape(tiles_across, tiles_down, TS, TS)
        .transpose(0, 2, 1, 3)
        .reshape(strip_width * strip_height)
    )
    sea_cells = mask_strip.reshape(strip_width * strip_height)
    targets = jnp.where(sea_cells == 1, columns, owner_count * PCAP)
    cell_numbers = jnp.arange(strip_width * strip_height)
    slot_cell = (
        jnp.zeros((owner_count * PCAP,), jnp.int32).at[targets].set(cell_numbers, mode="drop")
    )
    filled = (
        jnp.zeros((owner_count * PCAP,), jnp.int32)
        .at[targets]
        .set(jnp.ones_like(cell_numbers), mode="drop")
    )
    return (columns, sea_cells, slot_cell, filled)


def local(
    spectrum, wind_speed, wind_dir, freq_kernel, dir_kernel, depth, current, land_mask, tile_owner
):
    owner_count = lax.axis_size("comp") * lax.axis_size("sub")
    group_size = -(-K // owner_count)
    padded_count = group_size * owner_count
    strip_width, strip_height = land_mask.shape
    columns, sea_cells, slot_cell, filled = layout_maps(land_mask, tile_owner[0], owner_count)
    rim_width = 2
    cell_stack = jnp.stack([depth, current[0], current[1], land_mask.astype(jnp.float32)])
    fields = padded(cell_stack.astype(jnp.bfloat16), (("tile", 1),), rim_width).astype(
        cell_stack.dtype
    )
    source = source_terms(spectrum[0, 0], wind_speed[0, 0], wind_dir[0, 0], freq_kernel, dir_kernel)
    outgoing = jnp.pad(source, ((0, padded_count - K), (0, 0)))
    arrived = lax.all_to_all(outgoing, ("comp", "sub"), split_axis=0, concat_axis=1, tiled=True)
    gathered = jnp.take(arrived, columns, axis=1, mode="clip")
    density = jnp.where(sea_cells[None, :] == 1, gathered.astype(jnp.float32), 0.0).reshape(
        group_size, strip_width, strip_height
    )
    group_index = lax.axis_index("comp") * lax.axis_size("sub") + lax.axis_index("sub")
    component = group_index * group_size + jnp.arange(group_size)
    frequency = frequencies(NF)[jnp.minimum(component // ND, NF - 1)]
    comp_angle = directions(ND)[component % ND]
    metric = row_metric(strip_height)
    group_vel = group_speed(frequency[:, None, None], fields[0][None])
    along_x = (
        (group_vel * jnp.cos(comp_angle)[:, None, None] + fields[1][None])
        * TIME_STEP
        / (CELL_SIZE * metric[None, None, :])
    )
    along_y = (
        (group_vel * jnp.sin(comp_angle)[:, None, None] + fields[2][None]) * TIME_STEP / CELL_SIZE
    )
    sea_field = fields[3][None]
    total_width = strip_width + 2 * rim_width
    inner_y = window(along_y, 2, total_width - 2, 1)
    inner_sea = window(sea_field, 2, total_width - 2, 1)
    for substep in range(NSUB):
        extended = padded(density, (("tile", 1),), 2)
        density = upwind_sweep(extended, along_x, sea_field, 1)
        density = column_sweep(density, inner_y, inner_sea)
    leaving = density.astype(jnp.bfloat16).reshape(group_size, strip_width * strip_height)
    picked = jnp.take(leaving, slot_cell, axis=1, mode="clip")
    picked = jnp.where(filled[None, :] == 1, picked, jnp.zeros((), jnp.bfloat16))
    returned = lax.all_to_all(picked, ("comp", "sub"), split_axis=1, concat_axis=0, tiled=True)
    return returned[:K].reshape(1, 1, K, PCAP)


OWNERS = 8
STRIPS = 2
GROUP = OWNERS * STRIPS
RANKS = 4
ROWS = 80
EXTRA = 16
CAP = ROWS + EXTRA
LAST = GROUP - 1
PARTS = ((0, 48), (48, 32))
PART_ROWS = 48
WIDE = 32
TALL = 128
FIELD_ROWS = 72


def butterfly(values, pieces):
    for bit in range(3):
        step = 1 << bit
        odd = (pieces & step) != 0
        values = [jnp.where(odd, values[(j + step) % 8], values[j]) for j in range(8)]
    return values


def turn(values, by):
    by %= values.shape[0]
    if by == 0:
        return values
    return jnp.concatenate([values[-by:], values[:-by]], axis=0)


def first_sweep(d, face, bend):
    ahead = turn(d, -1)
    slope = ahead - d
    second = slope - turn(slope, 1)
    upstream = jnp.where(face > 0.0, second, turn(second, -1))
    flux = face * (0.5 * (d + ahead) - 0.5 * face * slope - bend * upstream)
    return d - (flux - turn(flux, 1))


def second_sweep(d, face, bend, lane):
    shape = d.shape
    flat = lambda v: v.reshape(shape[0] * shape[1], shape[2])
    d, face, bend = flat(d), flat(face), flat(bend)
    ahead = jnp.where(lane == TALL - 1, 0.0, pltpu.roll(d, TALL - 1, 1))
    slope = ahead - d
    second = slope - jnp.where(lane == 0, d, pltpu.roll(slope, 1, 1))
    upstream = jnp.where(face > 0.0, second, pltpu.roll(second, TALL - 1, 1))
    flux = face * (0.5 * (d + ahead) - 0.5 * face * slope - bend * upstream)
    return (d - (flux - pltpu.roll(flux, 1, 1))).reshape(shape)


def exchange_kernel(
    source_ref, depth_ref, current_ref, mask_ref, owner_ref, out_ref, place_ref,
    packed, arrived, fields, density, leaving, first_rate, second_rate, drift, tile_map,
    field_ref, angle_ref,
    go_send, go_recv, go_extra_send, go_extra_recv,
    back_send, back_recv, back_extra_send, back_extra_recv, field_send, field_recv,
):
    comp, tile, sub = lax.axis_index("comp"), lax.axis_index("tile"), lax.axis_index("sub")
    me = tile * OWNERS + comp * 2 + sub

    def partner(dc, dt, ds):
        c, t, s = lax.rem(comp + dc, 4), lax.rem(tile + dt, 2), lax.rem(sub + ds, 2)
        return t * OWNERS + c * 2 + s, {"comp": c, "tile": t, "sub": s}

    turns = [(dc, dt, ds) for dc in (2, 1, 3, 0) for dt in (0, 1) for ds in (0, 1)]
    turns = [item for item in turns if item != (0, 0, 0)]
    partners = [partner(*item) for item in turns]
    final_device = {"comp": 3, "tile": 1, "sub": 1}

    barrier = pltpu.get_barrier_semaphore()
    for _, where in partners:
        pl.semaphore_signal(barrier, inc=1, device_id=where, device_id_type=pl.DeviceIdType.MESH)
    pl.semaphore_wait(barrier, GROUP - 1)

    def remote(src, dst, send, recv, where):
        return pltpu.make_async_remote_copy(
            src_ref=src, dst_ref=dst, send_sem=send, recv_sem=recv,
            device_id=where, device_id_type=pl.DeviceIdType.MESH,
        )

    def iota(shape, dim):
        return lax.broadcasted_iota(jnp.int32, shape, dim)

    def number(condition):
        return jnp.where(condition, 1.0, 0.0)

    tiles = 2 * TALL // TS
    owners = owner_ref[...].astype(jnp.float32)
    owner_rows = jnp.broadcast_to(owners, (tiles, tiles))
    eye = iota((tiles, tiles), 0) == iota((tiles, tiles), 1)
    owner_column = jnp.sum(jnp.where(eye, owner_rows, 0.0), axis=1, keepdims=True)
    earlier = (owner_column == owner_rows) & (iota((tiles, tiles), 0) < iota((tiles, tiles), 1))
    rank = jnp.sum(number(earlier), axis=0, keepdims=True)
    column = iota((tiles, 256), 1)
    spread_tile = number(lax.shift_right_logical(column, 3) == iota((tiles, 256), 0))
    target = jnp.dot(owners * 32.0 + rank * 8.0, spread_tile, preferred_element_type=jnp.float32)
    target = target + (iota((1, 256), 1) & 7).astype(jnp.float32)
    field_ref[pl.ds(0, 16), :] = depth_ref[...]
    field_ref[pl.ds(16, 16), :] = current_ref[0]
    field_ref[pl.ds(32, 16), :] = current_ref[1]
    field_ref[pl.ds(48, 16), :] = mask_ref[...].astype(jnp.float32)
    field_ref[pl.ds(64, 1), :] = target[:, :TALL]
    field_ref[pl.ds(65, 1), :] = target[:, TALL:]
    field_ref[pl.ds(66, 6), :] = jnp.zeros((6, TALL), jnp.float32)
    beside = partner(0, 1, 0)[1]
    field_copy = remote(field_ref, fields.at[tile], field_send, field_recv, beside)
    field_copy.start()

    mine_owner = comp * 2 + sub
    wanted = (owner_column == mine_owner.astype(jnp.float32))
    rank_column = jnp.sum(jnp.where(eye, jnp.broadcast_to(rank, (tiles, tiles)), 0.0), axis=1, keepdims=True)
    lane_rank = lax.shift_right_logical(iota((1, 256), 1), 3) & 3
    held = wanted & (rank_column == lane_rank.astype(jnp.float32))
    tile_of = jnp.sum(jnp.where(held, iota((tiles, 256), 0).astype(jnp.float32), 0.0), axis=0, keepdims=True)
    tile_of = tile_of.astype(jnp.int32)

    def cell_x(at):
        return (lax.shift_right_logical(at, 5) - mine_owner) & 7

    def order(at):
        return (lax.shift_right_logical(at, 3) & 3) * 64 + cell_x(at) * 8 + (at & 7)

    lanes = iota((1, 256), 1)
    column_y = (tile_of & 15) * 8 + (lanes & 7)
    column_x = lax.shift_right_logical(tile_of, 4) * 8 + cell_x(lanes)
    pick = number(iota((TALL, 256), 0) == column_y)
    by_x = jnp.dot(mask_ref[...].astype(jnp.float32), pick, preferred_element_type=jnp.float32)
    mine = jnp.sum(jnp.where(iota((16, 256), 0) == column_x, by_x, 0.0), axis=0, keepdims=True)
    before = number(order(iota((256, 256), 0)) < order(iota((256, 256), 1)))
    slot = jnp.dot(jnp.broadcast_to(mine, (8, 256)), before, preferred_element_type=jnp.float32)[:1]
    slot = jnp.where(mine > 0.5, slot, -1.0).astype(jnp.int32)
    place_ref[...] = number(iota((256, 256), 0) == slot).astype(jnp.bfloat16)

    packed[...] = jnp.dot(
        source_ref[...], place_ref[...], preferred_element_type=jnp.float32
    ).astype(jnp.bfloat16)

    def aligned(value):
        return pl.multiple_of(value, 16)

    def go(part, number, where):
        at, rows = PARTS[part]
        return remote(
            packed.at[pl.ds(aligned(number * ROWS + at), rows)],
            arrived.at[me, pl.ds(at, rows)],
            go_send.at[part, number], go_recv.at[part, me], where,
        )

    def go_landed(part, number, where):
        at, rows = PARTS[part]
        spot = arrived.at[number, pl.ds(at, rows)]
        return remote(spot, spot, go_send.at[part, number], go_recv.at[part, number], where)

    def go_extra():
        return remote(
            packed.at[pl.ds(GROUP * ROWS, EXTRA)], arrived.at[me, pl.ds(ROWS, EXTRA)],
            go_extra_send, go_extra_recv.at[me], final_device,
        )

    for part in range(len(PARTS)):
        for number, where in partners:
            go(part, number, where).start()

    @pl.when(me != LAST)
    def _():
        go_extra().start()

    arrived[me, pl.ds(0, ROWS)] = packed[pl.ds(aligned(me * ROWS), ROWS), :]

    @pl.when(me == LAST)
    def _():
        arrived[LAST, pl.ds(ROWS, EXTRA)] = packed[pl.ds(GROUP * ROWS, EXTRA), :]

    @pl.when(me != LAST)
    def _():
        for number in range(GROUP):
            arrived[number, pl.ds(ROWS, EXTRA)] = jnp.zeros((EXTRA, 256), jnp.bfloat16)

    fields[tile] = field_ref[...]
    field_copy.wait()

    lane = lax.broadcasted_iota(jnp.int32, (1, TALL), 1)
    row_number = lax.broadcasted_iota(jnp.int32, (256, TALL), 0)
    for strip in range(STRIPS):
        for half in range(2):
            target = fields[strip, pl.ds(64 + half, 1), :].astype(jnp.int32)
            tile_map[strip, :, pl.ds(half * TALL, TALL)] = jnp.where(
                row_number == target, 1.0, 0.0
            ).astype(jnp.bfloat16)

    def whole(at):
        return jnp.concatenate([fields[strip, pl.ds(at, 16), :] for strip in range(STRIPS)], axis=0)

    depth, along_u, along_v, sea = whole(0), whole(16), whole(32), whole(48)
    above = lambda v: jnp.concatenate([v[1:], v[:1]], axis=0)
    beyond = lambda v: jnp.where(lane == TALL - 1, 0.0, pltpu.roll(v, TALL - 1, 1))
    latitude = LAT_EDGE * (2.0 * (lane.astype(jnp.float32) + 0.5) / TALL - 1.0)
    step_x = TIME_STEP / (CELL_SIZE * jnp.cos(latitude))
    half_x = 0.5 * step_x * sea * above(sea)
    half_y = 0.5 * (TIME_STEP / CELL_SIZE) * sea * beyond(sea)

    def spread(ref, at, value):
        for x in range(WIDE):
            ref[at, x] = jnp.broadcast_to(value[x : x + 1, :], (8, TALL))

    spread(drift, 0, half_x * (along_u + above(along_u)))
    spread(drift, 1, half_y * (along_v + beyond(along_v)))
    base = me * ROWS
    first_index = base // ND
    component = base + iota((CAP, TALL), 0)
    direction = component - ND * lax.shift_right_logical(component * 1821, 16)
    angle = (2.0 * math.pi / ND) * (direction.astype(jnp.float32) + 0.5)
    angle_ref[0] = jnp.cos(angle)
    angle_ref[1] = jnp.sin(angle)
    for which in range(4):
        index = jnp.minimum(first_index + which, NF - 1).astype(jnp.float32)
        exponent = jnp.broadcast_to(index * math.log(FREQ_RATIO), (1, TALL))
        frequency = FREQ_BASE * jnp.exp(exponent)
        angular = 2.0 * math.pi * frequency
        deep_number = angular * angular / GRAVITY
        wavenumber = deep_number / jnp.sqrt(jnp.tanh(deep_number * depth))
        relative = jnp.minimum(wavenumber * depth, KH_LIMIT)
        sinh = 0.5 * (jnp.exp(2.0 * relative) - jnp.exp(-2.0 * relative))
        speed = (0.5 + relative / sinh) * angular / wavenumber
        spread(first_rate, which, half_x * (speed + above(speed)))
        spread(second_rate, which, half_y * (speed + beyond(speed)))

    pieces = lax.shift_right_logical(lax.broadcasted_iota(jnp.int32, (1, 256), 1), 5)
    row8 = lax.broadcasted_iota(jnp.int32, (8, TALL), 0)
    wide_lane = lax.broadcasted_iota(jnp.int32, (WIDE * 8, TALL), 1)

    def back(part, number, where):
        at, rows = PARTS[part]
        return remote(
            leaving.at[number, pl.ds(at, rows)],
            out_ref.at[pl.ds(aligned(me * ROWS + at), rows)],
            back_send.at[part, number], back_recv.at[part, me], where,
        )

    def back_landed(part, number, where):
        at, rows = PARTS[part]
        spot = out_ref.at[pl.ds(aligned(number * ROWS + at), rows)]
        return remote(spot, spot, back_send.at[part, number], back_recv.at[part, number], where)

    def back_extra(number, where):
        return remote(
            leaving.at[number, pl.ds(ROWS, EXTRA)], out_ref.at[pl.ds(GROUP * ROWS, EXTRA)],
            back_extra_send.at[number], back_extra_recv, where,
        )

    for part in range(len(PARTS)):
        at, rows = PARTS[part]
        for number, where in partners:
            go_landed(part, number, where).wait_recv()
        if part == 1:

            @pl.when(me == LAST)
            def _():
                for number, where in partners:
                    spot = arrived.at[number, pl.ds(ROWS, EXTRA)]
                    remote(spot, spot, go_extra_send, go_extra_recv.at[number], where).wait_recv()

        for strip in range(STRIPS):
            blocks = [
                arrived[strip * OWNERS + o, pl.ds(at, PART_ROWS), :].astype(jnp.float32)
                for o in range(OWNERS)
            ]
            blocks = butterfly(blocks, pieces)
            lined = []
            for xx in range(TS):
                block = blocks[-xx % 8]
                if xx:
                    block = pltpu.roll(block, 256 - 32 * xx, 1)
                lined.append(block.astype(jnp.bfloat16))
            placed = jnp.dot(
                jnp.concatenate(lined, axis=0), tile_map[strip], preferred_element_type=jnp.float32
            )
            for xx in range(TS):
                for half in range(2):
                    density[strip * 16 + half * TS + xx] = placed[
                        xx * PART_ROWS : (xx + 1) * PART_ROWS, half * TALL : (half + 1) * TALL
                    ]

        def chunk(step, carry):
            start = base + at + step * 8
            index = start // ND
            table = index - first_index
            later = jnp.minimum(table + 1, 3)
            new = row8 >= (index + 1) * ND - start
            here = pl.ds(pl.multiple_of(step * 8, 8), 8)
            angle_at = pl.ds(pl.multiple_of(at + step * 8, 8), 8)
            cos, sin = angle_ref[0, angle_at, :], angle_ref[1, angle_at, :]
            face_x = jnp.where(new[None], first_rate[later], first_rate[table]) * cos[None] + drift[0]
            face_y = jnp.where(new[None], second_rate[later], second_rate[table]) * sin[None] + drift[1]
            bend_x = (1.0 - face_x * face_x) * (1.0 / 6.0)
            bend_y = (1.0 - face_y * face_y) * (1.0 / 6.0)
            d = density[:, here, :]
            for substep in range(NSUB):
                d = first_sweep(d, face_x, bend_x)
                d = second_sweep(d, face_y, bend_y, wide_lane)
            density[:, here, :] = d
            return carry

        count = PART_ROWS // 8 if part == 0 else jnp.where(me == LAST, PART_ROWS // 8, rows // 8)
        lax.fori_loop(0, count, chunk, 0)

        for strip in range(STRIPS):
            lined = [
                jnp.concatenate(
                    [density[strip * 16 + xx], density[strip * 16 + TS + xx]], axis=1
                ).astype(jnp.bfloat16)
                for xx in range(TS)
            ]
            sorted_rows = lax.dot_general(
                jnp.concatenate(lined, axis=0), tile_map[strip], (((1,), (1,)), ((), ())),
                preferred_element_type=jnp.float32,
            )
            blocks = []
            for xx in range(TS):
                block = sorted_rows[xx * PART_ROWS : (xx + 1) * PART_ROWS]
                blocks.append(pltpu.roll(block, 32 * xx, 1) if xx else block)
            blocks = butterfly(blocks, pieces)
            for o in range(OWNERS):
                leaving[strip * OWNERS + o, pl.ds(at, PART_ROWS)] = blocks[-o % 8].astype(jnp.bfloat16)

        for number, where in partners:
            back(part, number, where).start()
        if part == 1:

            @pl.when(me == LAST)
            def _():
                for number, where in partners:
                    back_extra(number, where).start()

    out_ref[pl.ds(aligned(me * ROWS), ROWS), :] = leaving[me, pl.ds(0, ROWS), :]

    @pl.when(me == LAST)
    def _():
        out_ref[pl.ds(GROUP * ROWS, EXTRA), :] = leaving[LAST, pl.ds(ROWS, EXTRA), :]

    for part in range(len(PARTS)):
        for number, where in partners:
            go(part, number, where).wait_send()
            back(part, number, where).wait_send()
            back_landed(part, number, where).wait_recv()

    @pl.when(me != LAST)
    def _():
        go_extra().wait_send()
        spot = out_ref.at[pl.ds(GROUP * ROWS, EXTRA)]
        remote(spot, spot, back_extra_send.at[LAST], back_extra_recv, final_device).wait_recv()

    @pl.when(me == LAST)
    def _():
        for number, where in partners:
            back_extra(number, where).wait_send()


def exchange(source, depth, current, land_mask, tile_owner):
    dma = pltpu.SemaphoreType.DMA
    vmem = pl.BlockSpec(memory_space=pltpu.VMEM)
    return pl.pallas_call(
        exchange_kernel,
        out_shape=[
            jax.ShapeDtypeStruct((K, 256), jnp.bfloat16),
            jax.ShapeDtypeStruct((256, 256), jnp.bfloat16),
        ],
        in_specs=[vmem] * 5,
        out_specs=[vmem] * 2,
        scratch_shapes=[
            pltpu.VMEM((K, 256), jnp.bfloat16),
            pltpu.VMEM((GROUP, CAP, 256), jnp.bfloat16),
            pltpu.VMEM((STRIPS, FIELD_ROWS, TALL), jnp.float32),
            pltpu.VMEM((WIDE, PART_ROWS, TALL), jnp.float32),
            pltpu.VMEM((GROUP, CAP, 256), jnp.bfloat16),
            pltpu.VMEM((4, WIDE, 8, TALL), jnp.float32),
            pltpu.VMEM((4, WIDE, 8, TALL), jnp.float32),
            pltpu.VMEM((2, WIDE, 8, TALL), jnp.float32),
            pltpu.VMEM((STRIPS, 256, 256), jnp.bfloat16),
            pltpu.VMEM((FIELD_ROWS, TALL), jnp.float32),
            pltpu.VMEM((2, CAP, TALL), jnp.float32),
            dma((2, GROUP)), dma((2, GROUP)), dma, dma((GROUP,)),
            dma((2, GROUP)), dma((2, GROUP)), dma((GROUP,)), dma, dma, dma,
        ],
        compiler_params=pltpu.CompilerParams(
            collective_id=0, has_side_effects=True, vmem_limit_bytes=40 * 1024 * 1024
        ),
    )(source, depth, current, land_mask, tile_owner)


def grouped(
    spectrum, wind_speed, wind_dir, freq_kernel, dir_kernel, depth, current, land_mask, tile_owner
):
    source = source_terms(spectrum[0, 0], wind_speed[0, 0], wind_dir[0, 0], freq_kernel, dir_kernel)
    returned, place = exchange(source, depth, current, land_mask, tile_owner)
    result = lax.dot_general(
        returned, place, (((1,), (1,)), ((), ())), preferred_element_type=jnp.float32
    ).astype(jnp.bfloat16)
    return result.reshape(1, 1, K, PCAP)


def solution(mesh):
    sizes = mesh.shape
    fits = (sizes["comp"], sizes["sub"], sizes["tile"]) == (4, 2, STRIPS)
    placed = (
        P(("ens", "tile"), ("comp", "sub"), None, None),
        P(("ens", "tile"), ("comp", "sub"), None),
        P(("ens", "tile"), ("comp", "sub"), None),
        P(),
        P(),
        P("tile", None),
        P(None, "tile", None),
        P("tile", None),
        P("tile", None),
    )
    return jax.shard_map(
        grouped if fits else local,
        mesh=mesh,
        in_specs=placed,
        out_specs=P(("ens", "tile"), ("comp", "sub"), None, None),
        check_vma=False,
    )
```

```python
import math

import jax
import jax.numpy as jnp
from jax import lax
from jax.experimental import pallas as pl
from jax.experimental.pallas import tpu as pltpu
from jax.sharding import PartitionSpec as P

NF = 36
ND = 36
TS = 8
NSUB = 2
K = 1296
PCAP = 256


GRAVITY = 9.81
FREQ_BASE = 0.035
FREQ_RATIO = 1.1
TIME_STEP = 450.0
CELL_SIZE = 27750.0
LAT_EDGE = 64.0 * math.pi / 180.0
WIND_RATE = 0.1
BREAK_RATE = 0.15
ENERGY_REF = 1.5
TRANSFER_RATE = 0.2
KH_LIMIT = 10.0


def padded(value, sides, width):
    for axis, dim in sides:
        devices, length = (lax.axis_size(axis), value.shape[dim])
        up = [(i, (i + 1) % devices) for i in range(devices)]
        down = [(j, i) for i, j in up]
        last = lax.slice_in_dim(value, length - width, length, axis=dim)
        leading = lax.slice_in_dim(value, 0, width, axis=dim)
        before = lax.ppermute(last, axis, up)
        after = lax.ppermute(leading, axis, down)
        value = jnp.concatenate([before, value, after], axis=dim)
    return value


def frequencies(how_many):
    return FREQ_BASE * jnp.power(jnp.float32(FREQ_RATIO), jnp.arange(how_many).astype(jnp.float32))


def directions(how_many):
    return 2.0 * math.pi * (jnp.arange(how_many).astype(jnp.float32) + 0.5) / how_many


def row_metric(rows_total):
    latitude = LAT_EDGE * (
        2.0 * (jnp.arange(rows_total).astype(jnp.float32) + 0.5) / rows_total - 1.0
    )
    return jnp.cos(latitude)


def group_speed(frequency, sea_depth):
    angular = 2.0 * math.pi * frequency
    deep_number = angular * angular / GRAVITY
    wavenumber = deep_number / jnp.sqrt(jnp.tanh(deep_number * sea_depth))
    relative = jnp.minimum(wavenumber * sea_depth, KH_LIMIT)
    group_ratio = 0.5 + relative / jnp.sinh(2.0 * relative)
    return group_ratio * angular / wavenumber


def source_terms(spectrum_block, wind_speed, heading, freq_kernel, dir_kernel):
    freq_count = freq_kernel.shape[0]
    dir_count = dir_kernel.shape[0]
    points = spectrum_block.shape[1]
    energy = spectrum_block.astype(jnp.float32).reshape(freq_count, dir_count, points)
    frequency = frequencies(freq_count)
    angles = directions(dir_count)
    weighted = jnp.sum(energy, axis=1) * frequency[:, None]
    first_moment = jnp.sum(weighted, axis=0)
    total = FREQ_BASE * sum(FREQ_RATIO**i for i in range(freq_count))
    mean_energy = first_moment / (dir_count * total)
    mean_freq = jnp.sum(weighted * frequency[:, None], axis=0) / first_moment
    phase_speed = GRAVITY / (2.0 * math.pi * frequency)
    forcing = (
        wind_speed[None, None, :]
        / phase_speed[:, None, None]
        * (
            jnp.cos(angles)[None, :, None] * jnp.cos(heading)[None, None, :]
            + jnp.sin(angles)[None, :, None] * jnp.sin(heading)[None, None, :]
        )
        - 1.0
    )
    growth = WIND_RATE * jnp.maximum(forcing, 0.0)
    damping = (
        BREAK_RATE
        * (frequency[:, None, None] / mean_freq[None, None, :])
        * jnp.square(mean_energy / ENERGY_REF)[None, None, :]
    )
    coupled = jnp.einsum("ab,bjp->ajp", freq_kernel, energy, precision=lax.Precision.HIGH)
    coupled = jnp.einsum("cj,ajp->acp", dir_kernel, coupled, precision=lax.Precision.HIGH)
    transfer = TRANSFER_RATE * energy * coupled / mean_energy[None, None, :]
    updated = (energy + growth * energy + transfer) / (1.0 + damping)
    return updated.reshape(freq_count * dir_count, points).astype(jnp.bfloat16)


def window(values, begin_at, end_at, along):
    return lax.slice_in_dim(values, begin_at, end_at, axis=along)


def upwind_sweep(density, courant, sea_mask, along):
    length = density.shape[along]
    behind = window(density, 0, length - 3, along)
    centre = window(density, 1, length - 2, along)
    ahead_one = window(density, 2, length - 1, along)
    beyond = window(density, 3, length, along)
    face_courant = 0.5 * (
        window(courant, 1, length - 2, along) + window(courant, 2, length - 1, along)
    )
    face_courant = (
        face_courant
        * window(sea_mask, 1, length - 2, along)
        * window(sea_mask, 2, length - 1, along)
    )
    curvature = (1.0 - face_courant * face_courant) / 6.0
    middle = 0.5 * (centre + ahead_one) - 0.5 * face_courant * (ahead_one - centre)
    upstream = jnp.where(
        face_courant > 0.0, ahead_one - 2.0 * centre + behind, beyond - 2.0 * ahead_one + centre
    )
    face_flux = face_courant * (middle - curvature * upstream)
    return window(density, 2, length - 2, along) - (
        window(face_flux, 1, length - 3, along) - window(face_flux, 0, length - 4, along)
    )


def column_sweep(density, courant, sea_mask):
    widths = ((0, 0), (0, 0), (2, 2))
    return upwind_sweep(
        jnp.pad(density, widths), jnp.pad(courant, widths), jnp.pad(sea_mask, widths), 2
    )


def layout_maps(mask_strip, owners, owner_count):
    strip_width, strip_height = mask_strip.shape
    tiles_across = strip_width // TS
    tiles_down = strip_height // TS
    tile_cells = (
        mask_strip.reshape(tiles_across, TS, tiles_down, TS)
        .transpose(0, 2, 1, 3)
        .reshape(tiles_across * tiles_down, TS * TS)
    )
    counts = jnp.sum(tile_cells, axis=1)
    tile_index = jnp.arange(tiles_across * tiles_down)
    earlier = (owners[None, :] == owners[:, None]) & (tile_index[None, :] < tile_index[:, None])
    offsets = jnp.sum(jnp.where(earlier, counts[None, :], 0), axis=1)
    rank_within = jnp.cumsum(tile_cells, axis=1) - tile_cells
    columns = owners[:, None] * PCAP + offsets[:, None] + rank_within
    columns = (
        columns.reshape(tiles_across, tiles_down, TS, TS)
        .transpose(0, 2, 1, 3)
        .reshape(strip_width * strip_height)
    )
    sea_cells = mask_strip.reshape(strip_width * strip_height)
    targets = jnp.where(sea_cells == 1, columns, owner_count * PCAP)
    cell_numbers = jnp.arange(strip_width * strip_height)
    slot_cell = (
        jnp.zeros((owner_count * PCAP,), jnp.int32).at[targets].set(cell_numbers, mode="drop")
    )
    filled = (
        jnp.zeros((owner_count * PCAP,), jnp.int32)
        .at[targets]
        .set(jnp.ones_like(cell_numbers), mode="drop")
    )
    return (columns, sea_cells, slot_cell, filled)


def local(
    spectrum, wind_speed, wind_dir, freq_kernel, dir_kernel, depth, current, land_mask, tile_owner
):
    owner_count = lax.axis_size("comp") * lax.axis_size("sub")
    group_size = -(-K // owner_count)
    padded_count = group_size * owner_count
    strip_width, strip_height = land_mask.shape
    columns, sea_cells, slot_cell, filled = layout_maps(land_mask, tile_owner[0], owner_count)
    rim_width = 2
    cell_stack = jnp.stack([depth, current[0], current[1], land_mask.astype(jnp.float32)])
    fields = padded(cell_stack.astype(jnp.bfloat16), (("tile", 1),), rim_width).astype(
        cell_stack.dtype
    )
    source = source_terms(spectrum[0, 0], wind_speed[0, 0], wind_dir[0, 0], freq_kernel, dir_kernel)
    outgoing = jnp.pad(source, ((0, padded_count - K), (0, 0)))
    arrived = lax.all_to_all(outgoing, ("comp", "sub"), split_axis=0, concat_axis=1, tiled=True)
    gathered = jnp.take(arrived, columns, axis=1, mode="clip")
    density = jnp.where(sea_cells[None, :] == 1, gathered.astype(jnp.float32), 0.0).reshape(
        group_size, strip_width, strip_height
    )
    group_index = lax.axis_index("comp") * lax.axis_size("sub") + lax.axis_index("sub")
    component = group_index * group_size + jnp.arange(group_size)
    frequency = frequencies(NF)[jnp.minimum(component // ND, NF - 1)]
    comp_angle = directions(ND)[component % ND]
    metric = row_metric(strip_height)
    group_vel = group_speed(frequency[:, None, None], fields[0][None])
    along_x = (
        (group_vel * jnp.cos(comp_angle)[:, None, None] + fields[1][None])
        * TIME_STEP
        / (CELL_SIZE * metric[None, None, :])
    )
    along_y = (
        (group_vel * jnp.sin(comp_angle)[:, None, None] + fields[2][None]) * TIME_STEP / CELL_SIZE
    )
    sea_field = fields[3][None]
    total_width = strip_width + 2 * rim_width
    inner_y = window(along_y, 2, total_width - 2, 1)
    inner_sea = window(sea_field, 2, total_width - 2, 1)
    for substep in range(NSUB):
        extended = padded(density, (("tile", 1),), 2)
        density = upwind_sweep(extended, along_x, sea_field, 1)
        density = column_sweep(density, inner_y, inner_sea)
    leaving = density.astype(jnp.bfloat16).reshape(group_size, strip_width * strip_height)
    picked = jnp.take(leaving, slot_cell, axis=1, mode="clip")
    picked = jnp.where(filled[None, :] == 1, picked, jnp.zeros((), jnp.bfloat16))
    returned = lax.all_to_all(picked, ("comp", "sub"), split_axis=1, concat_axis=0, tiled=True)
    return returned[:K].reshape(1, 1, K, PCAP)


OWNERS = 8
STRIPS = 2
GROUP = OWNERS * STRIPS
RANKS = 4
ROWS = 80
EXTRA = 16
CAP = ROWS + EXTRA
LAST = GROUP - 1
PARTS = ((0, 32), (32, 32), (64, 16))
FINAL = len(PARTS) - 1
MOST_ROWS = max(PARTS[FINAL][1] + EXTRA, *(rows for _, rows in PARTS))
WIDE = 32
TALL = 128
FIELD_ROWS = 72


def butterfly(values, pieces):
    for bit in range(3):
        step = 1 << bit
        odd = (pieces & step) != 0
        values = [jnp.where(odd, values[(j + step) % 8], values[j]) for j in range(8)]
    return values


def turn(values, by):
    by %= values.shape[0]
    if by == 0:
        return values
    return jnp.concatenate([values[-by:], values[:-by]], axis=0)


def first_sweep(d, face, bend):
    ahead = turn(d, -1)
    slope = ahead - d
    second = slope - turn(slope, 1)
    upstream = jnp.where(face > 0.0, second, turn(second, -1))
    flux = face * (0.5 * (d + ahead) - 0.5 * face * slope - bend * upstream)
    return d - (flux - turn(flux, 1))


def second_sweep(d, face, bend, lane):
    shape = d.shape
    flat = lambda v: v.reshape(shape[0] * shape[1], shape[2])
    d, face, bend = flat(d), flat(face), flat(bend)
    ahead = jnp.where(lane == TALL - 1, 0.0, pltpu.roll(d, TALL - 1, 1))
    slope = ahead - d
    second = slope - jnp.where(lane == 0, d, pltpu.roll(slope, 1, 1))
    upstream = jnp.where(face > 0.0, second, pltpu.roll(second, TALL - 1, 1))
    flux = face * (0.5 * (d + ahead) - 0.5 * face * slope - bend * upstream)
    return (d - (flux - pltpu.roll(flux, 1, 1))).reshape(shape)


def exchange_kernel(
    source_ref, depth_ref, current_ref, mask_ref, owner_ref, out_ref, place_ref,
    packed, arrived, fields, density, leaving, first_rate, second_rate, drift, tile_map,
    field_ref, angle_ref,
    go_send, go_recv, go_extra_send, go_extra_recv,
    back_send, back_recv, back_extra_send, back_extra_recv, field_send, field_recv,
):
    comp, tile, sub = lax.axis_index("comp"), lax.axis_index("tile"), lax.axis_index("sub")
    me = tile * OWNERS + comp * 2 + sub

    def partner(dc, dt, ds):
        c, t, s = lax.rem(comp + dc, 4), lax.rem(tile + dt, 2), lax.rem(sub + ds, 2)
        return t * OWNERS + c * 2 + s, {"comp": c, "tile": t, "sub": s}

    turns = [(dc, dt, ds) for dc in (2, 1, 3, 0) for dt in (0, 1) for ds in (0, 1)]
    turns = [item for item in turns if item != (0, 0, 0)]
    partners = [partner(*item) for item in turns]
    final_device = {"comp": 3, "tile": 1, "sub": 1}

    barrier = pltpu.get_barrier_semaphore()
    for _, where in partners:
        pl.semaphore_signal(barrier, inc=1, device_id=where, device_id_type=pl.DeviceIdType.MESH)
    pl.semaphore_wait(barrier, GROUP - 1)

    def remote(src, dst, send, recv, where):
        return pltpu.make_async_remote_copy(
            src_ref=src, dst_ref=dst, send_sem=send, recv_sem=recv,
            device_id=where, device_id_type=pl.DeviceIdType.MESH,
        )

    def iota(shape, dim):
        return lax.broadcasted_iota(jnp.int32, shape, dim)

    def number(condition):
        return jnp.where(condition, 1.0, 0.0)

    tiles = 2 * TALL // TS
    owners = owner_ref[...].astype(jnp.float32)
    owner_rows = jnp.broadcast_to(owners, (tiles, tiles))
    eye = iota((tiles, tiles), 0) == iota((tiles, tiles), 1)
    owner_column = jnp.sum(jnp.where(eye, owner_rows, 0.0), axis=1, keepdims=True)
    earlier = (owner_column == owner_rows) & (iota((tiles, tiles), 0) < iota((tiles, tiles), 1))
    rank = jnp.sum(number(earlier), axis=0, keepdims=True)
    column = iota((tiles, 256), 1)
    spread_tile = number(lax.shift_right_logical(column, 3) == iota((tiles, 256), 0))
    target = jnp.dot(owners * 32.0 + rank * 8.0, spread_tile, preferred_element_type=jnp.float32)
    target = target + (iota((1, 256), 1) & 7).astype(jnp.float32)
    field_ref[pl.ds(0, 16), :] = depth_ref[...]
    field_ref[pl.ds(16, 16), :] = current_ref[0]
    field_ref[pl.ds(32, 16), :] = current_ref[1]
    field_ref[pl.ds(48, 16), :] = mask_ref[...].astype(jnp.float32)
    field_ref[pl.ds(64, 1), :] = target[:, :TALL]
    field_ref[pl.ds(65, 1), :] = target[:, TALL:]
    field_ref[pl.ds(66, 6), :] = jnp.zeros((6, TALL), jnp.float32)
    beside = partner(0, 1, 0)[1]
    field_copy = remote(field_ref, fields.at[tile], field_send, field_recv, beside)
    field_copy.start()

    mine_owner = comp * 2 + sub
    wanted = (owner_column == mine_owner.astype(jnp.float32))
    rank_column = jnp.sum(jnp.where(eye, jnp.broadcast_to(rank, (tiles, tiles)), 0.0), axis=1, keepdims=True)
    lane_rank = lax.shift_right_logical(iota((1, 256), 1), 3) & 3
    held = wanted & (rank_column == lane_rank.astype(jnp.float32))
    tile_of = jnp.sum(jnp.where(held, iota((tiles, 256), 0).astype(jnp.float32), 0.0), axis=0, keepdims=True)
    tile_of = tile_of.astype(jnp.int32)

    def cell_x(at):
        return (lax.shift_right_logical(at, 5) - mine_owner) & 7

    def order(at):
        return (lax.shift_right_logical(at, 3) & 3) * 64 + cell_x(at) * 8 + (at & 7)

    lanes = iota((1, 256), 1)
    column_y = (tile_of & 15) * 8 + (lanes & 7)
    column_x = lax.shift_right_logical(tile_of, 4) * 8 + cell_x(lanes)
    pick = number(iota((TALL, 256), 0) == column_y)
    by_x = jnp.dot(mask_ref[...].astype(jnp.float32), pick, preferred_element_type=jnp.float32)
    mine = jnp.sum(jnp.where(iota((16, 256), 0) == column_x, by_x, 0.0), axis=0, keepdims=True)
    before = number(order(iota((256, 256), 0)) < order(iota((256, 256), 1)))
    slot = jnp.dot(jnp.broadcast_to(mine, (8, 256)), before, preferred_element_type=jnp.float32)[:1]
    slot = jnp.where(mine > 0.5, slot, -1.0).astype(jnp.int32)
    place_ref[...] = number(iota((256, 256), 0) == slot).astype(jnp.bfloat16)

    packed[...] = jnp.dot(
        source_ref[...], place_ref[...], preferred_element_type=jnp.float32
    ).astype(jnp.bfloat16)

    def aligned(value):
        return pl.multiple_of(value, 16)

    def go(part, number, where):
        at, rows = PARTS[part]
        return remote(
            packed.at[pl.ds(aligned(number * ROWS + at), rows)],
            arrived.at[me, pl.ds(at, rows)],
            go_send.at[part, number], go_recv.at[part, me], where,
        )

    def go_landed(part, number, where):
        at, rows = PARTS[part]
        spot = arrived.at[number, pl.ds(at, rows)]
        return remote(spot, spot, go_send.at[part, number], go_recv.at[part, number], where)

    def go_extra():
        return remote(
            packed.at[pl.ds(GROUP * ROWS, EXTRA)], arrived.at[me, pl.ds(ROWS, EXTRA)],
            go_extra_send, go_extra_recv.at[me], final_device,
        )

    for part in range(len(PARTS)):
        for number, where in partners:
            go(part, number, where).start()

    @pl.when(me != LAST)
    def _():
        go_extra().start()

    arrived[me, pl.ds(0, ROWS)] = packed[pl.ds(aligned(me * ROWS), ROWS), :]

    @pl.when(me == LAST)
    def _():
        arrived[LAST, pl.ds(ROWS, EXTRA)] = packed[pl.ds(GROUP * ROWS, EXTRA), :]

    @pl.when(me != LAST)
    def _():
        for number in range(GROUP):
            arrived[number, pl.ds(ROWS, EXTRA)] = jnp.zeros((EXTRA, 256), jnp.bfloat16)

    fields[tile] = field_ref[...]
    field_copy.wait()

    lane = lax.broadcasted_iota(jnp.int32, (1, TALL), 1)
    row_number = lax.broadcasted_iota(jnp.int32, (256, TALL), 0)
    for strip in range(STRIPS):
        for half in range(2):
            target = fields[strip, pl.ds(64 + half, 1), :].astype(jnp.int32)
            tile_map[strip, :, pl.ds(half * TALL, TALL)] = jnp.where(
                row_number == target, 1.0, 0.0
            ).astype(jnp.bfloat16)

    def whole(at):
        return jnp.concatenate([fields[strip, pl.ds(at, 16), :] for strip in range(STRIPS)], axis=0)

    depth, along_u, along_v, sea = whole(0), whole(16), whole(32), whole(48)
    above = lambda v: jnp.concatenate([v[1:], v[:1]], axis=0)
    beyond = lambda v: jnp.where(lane == TALL - 1, 0.0, pltpu.roll(v, TALL - 1, 1))
    latitude = LAT_EDGE * (2.0 * (lane.astype(jnp.float32) + 0.5) / TALL - 1.0)
    step_x = TIME_STEP / (CELL_SIZE * jnp.cos(latitude))
    half_x = 0.5 * step_x * sea * above(sea)
    half_y = 0.5 * (TIME_STEP / CELL_SIZE) * sea * beyond(sea)

    def spread(ref, at, value):
        for x in range(WIDE):
            ref[at, x] = jnp.broadcast_to(value[x : x + 1, :], (8, TALL))

    spread(drift, 0, half_x * (along_u + above(along_u)))
    spread(drift, 1, half_y * (along_v + beyond(along_v)))
    base = me * ROWS
    first_index = base // ND
    component = base + iota((CAP, TALL), 0)
    direction = component - ND * lax.shift_right_logical(component * 1821, 16)
    angle = (2.0 * math.pi / ND) * (direction.astype(jnp.float32) + 0.5)
    angle_ref[0] = jnp.cos(angle)
    angle_ref[1] = jnp.sin(angle)
    for which in range(4):
        index = jnp.minimum(first_index + which, NF - 1).astype(jnp.float32)
        exponent = jnp.broadcast_to(index * math.log(FREQ_RATIO), (1, TALL))
        frequency = FREQ_BASE * jnp.exp(exponent)
        angular = 2.0 * math.pi * frequency
        deep_number = angular * angular / GRAVITY
        wavenumber = deep_number / jnp.sqrt(jnp.tanh(deep_number * depth))
        relative = jnp.minimum(wavenumber * depth, KH_LIMIT)
        sinh = 0.5 * (jnp.exp(2.0 * relative) - jnp.exp(-2.0 * relative))
        speed = (0.5 + relative / sinh) * angular / wavenumber
        spread(first_rate, which, half_x * (speed + above(speed)))
        spread(second_rate, which, half_y * (speed + beyond(speed)))

    pieces = lax.shift_right_logical(lax.broadcasted_iota(jnp.int32, (1, 256), 1), 5)
    row8 = lax.broadcasted_iota(jnp.int32, (8, TALL), 0)
    wide_lane = lax.broadcasted_iota(jnp.int32, (WIDE * 8, TALL), 1)

    def back(part, number, where):
        at, rows = PARTS[part]
        return remote(
            leaving.at[number, pl.ds(at, rows)],
            out_ref.at[pl.ds(aligned(me * ROWS + at), rows)],
            back_send.at[part, number], back_recv.at[part, me], where,
        )

    def back_landed(part, number, where):
        at, rows = PARTS[part]
        spot = out_ref.at[pl.ds(aligned(number * ROWS + at), rows)]
        return remote(spot, spot, back_send.at[part, number], back_recv.at[part, number], where)

    def back_extra(number, where):
        return remote(
            leaving.at[number, pl.ds(ROWS, EXTRA)], out_ref.at[pl.ds(GROUP * ROWS, EXTRA)],
            back_extra_send.at[number], back_extra_recv, where,
        )

    for part in range(len(PARTS)):
        at, rows = PARTS[part]
        height = rows + EXTRA if part == FINAL else rows
        for number, where in partners:
            go_landed(part, number, where).wait_recv()
        if part == FINAL:

            @pl.when(me == LAST)
            def _():
                for number, where in partners:
                    spot = arrived.at[number, pl.ds(ROWS, EXTRA)]
                    remote(spot, spot, go_extra_send, go_extra_recv.at[number], where).wait_recv()

        for strip in range(STRIPS):
            blocks = [
                arrived[strip * OWNERS + o, pl.ds(at, height), :].astype(jnp.float32)
                for o in range(OWNERS)
            ]
            blocks = butterfly(blocks, pieces)
            lined = []
            for xx in range(TS):
                block = blocks[-xx % 8]
                if xx:
                    block = pltpu.roll(block, 256 - 32 * xx, 1)
                lined.append(block.astype(jnp.bfloat16))
            placed = jnp.dot(
                jnp.concatenate(lined, axis=0), tile_map[strip], preferred_element_type=jnp.float32
            )
            for xx in range(TS):
                for half in range(2):
                    density[strip * 16 + half * TS + xx, pl.ds(0, height)] = placed[
                        xx * height : (xx + 1) * height, half * TALL : (half + 1) * TALL
                    ]

        def chunk(step, carry):
            start = base + at + step * 8
            index = start // ND
            table = index - first_index
            later = jnp.minimum(table + 1, 3)
            new = row8 >= (index + 1) * ND - start
            here = pl.ds(pl.multiple_of(step * 8, 8), 8)
            angle_at = pl.ds(pl.multiple_of(at + step * 8, 8), 8)
            cos, sin = angle_ref[0, angle_at, :], angle_ref[1, angle_at, :]
            face_x = jnp.where(new[None], first_rate[later], first_rate[table]) * cos[None] + drift[0]
            face_y = jnp.where(new[None], second_rate[later], second_rate[table]) * sin[None] + drift[1]
            bend_x = (1.0 - face_x * face_x) * (1.0 / 6.0)
            bend_y = (1.0 - face_y * face_y) * (1.0 / 6.0)
            d = density[:, here, :]
            for substep in range(NSUB):
                d = first_sweep(d, face_x, bend_x)
                d = second_sweep(d, face_y, bend_y, wide_lane)
            density[:, here, :] = d
            return carry

        count = rows // 8 if part < FINAL else jnp.where(me == LAST, height // 8, rows // 8)
        lax.fori_loop(0, count, chunk, 0)

        for strip in range(STRIPS):
            lined = [
                jnp.concatenate(
                    [density[strip * 16 + half * TS + xx, pl.ds(0, height)] for half in range(2)], axis=1
                ).astype(jnp.bfloat16)
                for xx in range(TS)
            ]
            sorted_rows = lax.dot_general(
                jnp.concatenate(lined, axis=0), tile_map[strip], (((1,), (1,)), ((), ())),
                preferred_element_type=jnp.float32,
            )
            blocks = []
            for xx in range(TS):
                block = sorted_rows[xx * height : (xx + 1) * height]
                blocks.append(pltpu.roll(block, 32 * xx, 1) if xx else block)
            blocks = butterfly(blocks, pieces)
            for o in range(OWNERS):
                leaving[strip * OWNERS + o, pl.ds(at, height)] = blocks[-o % 8].astype(jnp.bfloat16)

        for number, where in partners:
            back(part, number, where).start()
        if part == FINAL:

            @pl.when(me == LAST)
            def _():
                for number, where in partners:
                    back_extra(number, where).start()

    out_ref[pl.ds(aligned(me * ROWS), ROWS), :] = leaving[me, pl.ds(0, ROWS), :]

    @pl.when(me == LAST)
    def _():
        out_ref[pl.ds(GROUP * ROWS, EXTRA), :] = leaving[LAST, pl.ds(ROWS, EXTRA), :]

    for part in range(len(PARTS)):
        for number, where in partners:
            go(part, number, where).wait_send()
            back(part, number, where).wait_send()
            back_landed(part, number, where).wait_recv()

    @pl.when(me != LAST)
    def _():
        go_extra().wait_send()
        spot = out_ref.at[pl.ds(GROUP * ROWS, EXTRA)]
        remote(spot, spot, back_extra_send.at[LAST], back_extra_recv, final_device).wait_recv()

    @pl.when(me == LAST)
    def _():
        for number, where in partners:
            back_extra(number, where).wait_send()


def exchange(source, depth, current, land_mask, tile_owner):
    dma = pltpu.SemaphoreType.DMA
    vmem = pl.BlockSpec(memory_space=pltpu.VMEM)
    return pl.pallas_call(
        exchange_kernel,
        out_shape=[
            jax.ShapeDtypeStruct((K, 256), jnp.bfloat16),
            jax.ShapeDtypeStruct((256, 256), jnp.bfloat16),
        ],
        in_specs=[vmem] * 5,
        out_specs=[vmem] * 2,
        scratch_shapes=[
            pltpu.VMEM((K, 256), jnp.bfloat16),
            pltpu.VMEM((GROUP, CAP, 256), jnp.bfloat16),
            pltpu.VMEM((STRIPS, FIELD_ROWS, TALL), jnp.float32),
            pltpu.VMEM((WIDE, MOST_ROWS, TALL), jnp.float32),
            pltpu.VMEM((GROUP, CAP, 256), jnp.bfloat16),
            pltpu.VMEM((4, WIDE, 8, TALL), jnp.float32),
            pltpu.VMEM((4, WIDE, 8, TALL), jnp.float32),
            pltpu.VMEM((2, WIDE, 8, TALL), jnp.float32),
            pltpu.VMEM((STRIPS, 256, 256), jnp.bfloat16),
            pltpu.VMEM((FIELD_ROWS, TALL), jnp.float32),
            pltpu.VMEM((2, CAP, TALL), jnp.float32),
            dma((len(PARTS), GROUP)), dma((len(PARTS), GROUP)), dma, dma((GROUP,)),
            dma((len(PARTS), GROUP)), dma((len(PARTS), GROUP)), dma((GROUP,)), dma, dma, dma,
        ],
        compiler_params=pltpu.CompilerParams(
            collective_id=0, has_side_effects=True, vmem_limit_bytes=40 * 1024 * 1024
        ),
    )(source, depth, current, land_mask, tile_owner)


def grouped(
    spectrum, wind_speed, wind_dir, freq_kernel, dir_kernel, depth, current, land_mask, tile_owner
):
    source = source_terms(spectrum[0, 0], wind_speed[0, 0], wind_dir[0, 0], freq_kernel, dir_kernel)
    returned, place = exchange(source, depth, current, land_mask, tile_owner)
    result = lax.dot_general(
        returned, place, (((1,), (1,)), ((), ())), preferred_element_type=jnp.float32
    ).astype(jnp.bfloat16)
    return result.reshape(1, 1, K, PCAP)


def solution(mesh):
    sizes = mesh.shape
    fits = (sizes["comp"], sizes["sub"], sizes["tile"]) == (4, 2, STRIPS)
    placed = (
        P(("ens", "tile"), ("comp", "sub"), None, None),
        P(("ens", "tile"), ("comp", "sub"), None),
        P(("ens", "tile"), ("comp", "sub"), None),
        P(),
        P(),
        P("tile", None),
        P(None, "tile", None),
        P("tile", None),
        P("tile", None),
    )
    return jax.shard_map(
        grouped if fits else local,
        mesh=mesh,
        in_specs=placed,
        out_specs=P(("ens", "tile"), ("comp", "sub"), None, None),
        check_vma=False,
    )
```

```python
import math

import jax
import jax.numpy as jnp
from jax import lax
from jax.experimental import pallas as pl
from jax.experimental.pallas import tpu as pltpu
from jax.sharding import PartitionSpec as P

NF = 36
ND = 36
TS = 8
NSUB = 2
K = 1296
PCAP = 256


GRAVITY = 9.81
FREQ_BASE = 0.035
FREQ_RATIO = 1.1
TIME_STEP = 450.0
CELL_SIZE = 27750.0
LAT_EDGE = 64.0 * math.pi / 180.0
WIND_RATE = 0.1
BREAK_RATE = 0.15
ENERGY_REF = 1.5
TRANSFER_RATE = 0.2
KH_LIMIT = 10.0


def padded(value, sides, width):
    for axis, dim in sides:
        devices, length = (lax.axis_size(axis), value.shape[dim])
        up = [(i, (i + 1) % devices) for i in range(devices)]
        down = [(j, i) for i, j in up]
        last = lax.slice_in_dim(value, length - width, length, axis=dim)
        leading = lax.slice_in_dim(value, 0, width, axis=dim)
        before = lax.ppermute(last, axis, up)
        after = lax.ppermute(leading, axis, down)
        value = jnp.concatenate([before, value, after], axis=dim)
    return value


def frequencies(how_many):
    return FREQ_BASE * jnp.power(jnp.float32(FREQ_RATIO), jnp.arange(how_many).astype(jnp.float32))


def directions(how_many):
    return 2.0 * math.pi * (jnp.arange(how_many).astype(jnp.float32) + 0.5) / how_many


def row_metric(rows_total):
    latitude = LAT_EDGE * (
        2.0 * (jnp.arange(rows_total).astype(jnp.float32) + 0.5) / rows_total - 1.0
    )
    return jnp.cos(latitude)


def group_speed(frequency, sea_depth):
    angular = 2.0 * math.pi * frequency
    deep_number = angular * angular / GRAVITY
    wavenumber = deep_number / jnp.sqrt(jnp.tanh(deep_number * sea_depth))
    relative = jnp.minimum(wavenumber * sea_depth, KH_LIMIT)
    group_ratio = 0.5 + relative / jnp.sinh(2.0 * relative)
    return group_ratio * angular / wavenumber


def heading_parts(heading):
    quarter = 0.25 * heading
    square = quarter * quarter
    sine = 1.0 / 5040.0 - square / 362880.0
    sine = quarter * (1.0 - square * (1.0 / 6.0 - square * (1.0 / 120.0 - square * sine)))
    cosine = 1.0 / 720.0 - square * (1.0 / 40320.0 - square / 3628800.0)
    cosine = 1.0 - square * (0.5 - square * (1.0 / 24.0 - square * cosine))
    for _ in range(2):
        sine, cosine = 2.0 * sine * cosine, 1.0 - 2.0 * sine * sine
    return cosine, sine


def source_terms(spectrum_block, wind_speed, heading, freq_kernel, dir_kernel):
    freq_count = freq_kernel.shape[0]
    dir_count = dir_kernel.shape[0]
    points = spectrum_block.shape[1]
    energy = spectrum_block.astype(jnp.float32).reshape(freq_count, dir_count, points)
    frequency = frequencies(freq_count)
    angles = directions(dir_count)
    weighted = jnp.sum(energy, axis=1) * frequency[:, None]
    first_moment = jnp.sum(weighted, axis=0)
    total = FREQ_BASE * sum(FREQ_RATIO**i for i in range(freq_count))
    mean_energy = first_moment / (dir_count * total)
    mean_freq = jnp.sum(weighted * frequency[:, None], axis=0) / first_moment
    phase_speed = GRAVITY / (2.0 * math.pi * frequency)
    heading_cos, heading_sin = heading_parts(heading)
    forcing = (
        wind_speed[None, None, :]
        / phase_speed[:, None, None]
        * (
            jnp.cos(angles)[None, :, None] * heading_cos[None, None, :]
            + jnp.sin(angles)[None, :, None] * heading_sin[None, None, :]
        )
        - 1.0
    )
    growth = WIND_RATE * jnp.maximum(forcing, 0.0)
    damping = (
        BREAK_RATE
        * (frequency[:, None, None] / mean_freq[None, None, :])
        * jnp.square(mean_energy / ENERGY_REF)[None, None, :]
    )
    coupled = jnp.einsum("ab,bjp->ajp", freq_kernel, energy, precision=lax.Precision.HIGH)
    coupled = jnp.einsum("cj,ajp->acp", dir_kernel, coupled, precision=lax.Precision.HIGH)
    transfer = TRANSFER_RATE * energy * coupled / mean_energy[None, None, :]
    updated = (energy + growth * energy + transfer) / (1.0 + damping)
    return updated.reshape(freq_count * dir_count, points).astype(jnp.bfloat16)


def window(values, begin_at, end_at, along):
    return lax.slice_in_dim(values, begin_at, end_at, axis=along)


def upwind_sweep(density, courant, sea_mask, along):
    length = density.shape[along]
    behind = window(density, 0, length - 3, along)
    centre = window(density, 1, length - 2, along)
    ahead_one = window(density, 2, length - 1, along)
    beyond = window(density, 3, length, along)
    face_courant = 0.5 * (
        window(courant, 1, length - 2, along) + window(courant, 2, length - 1, along)
    )
    face_courant = (
        face_courant
        * window(sea_mask, 1, length - 2, along)
        * window(sea_mask, 2, length - 1, along)
    )
    curvature = (1.0 - face_courant * face_courant) / 6.0
    middle = 0.5 * (centre + ahead_one) - 0.5 * face_courant * (ahead_one - centre)
    upstream = jnp.where(
        face_courant > 0.0, ahead_one - 2.0 * centre + behind, beyond - 2.0 * ahead_one + centre
    )
    face_flux = face_courant * (middle - curvature * upstream)
    return window(density, 2, length - 2, along) - (
        window(face_flux, 1, length - 3, along) - window(face_flux, 0, length - 4, along)
    )


def column_sweep(density, courant, sea_mask):
    widths = ((0, 0), (0, 0), (2, 2))
    return upwind_sweep(
        jnp.pad(density, widths), jnp.pad(courant, widths), jnp.pad(sea_mask, widths), 2
    )


def layout_maps(mask_strip, owners, owner_count):
    strip_width, strip_height = mask_strip.shape
    tiles_across = strip_width // TS
    tiles_down = strip_height // TS
    tile_cells = (
        mask_strip.reshape(tiles_across, TS, tiles_down, TS)
        .transpose(0, 2, 1, 3)
        .reshape(tiles_across * tiles_down, TS * TS)
    )
    counts = jnp.sum(tile_cells, axis=1)
    tile_index = jnp.arange(tiles_across * tiles_down)
    earlier = (owners[None, :] == owners[:, None]) & (tile_index[None, :] < tile_index[:, None])
    offsets = jnp.sum(jnp.where(earlier, counts[None, :], 0), axis=1)
    rank_within = jnp.cumsum(tile_cells, axis=1) - tile_cells
    columns = owners[:, None] * PCAP + offsets[:, None] + rank_within
    columns = (
        columns.reshape(tiles_across, tiles_down, TS, TS)
        .transpose(0, 2, 1, 3)
        .reshape(strip_width * strip_height)
    )
    sea_cells = mask_strip.reshape(strip_width * strip_height)
    targets = jnp.where(sea_cells == 1, columns, owner_count * PCAP)
    cell_numbers = jnp.arange(strip_width * strip_height)
    slot_cell = (
        jnp.zeros((owner_count * PCAP,), jnp.int32).at[targets].set(cell_numbers, mode="drop")
    )
    filled = (
        jnp.zeros((owner_count * PCAP,), jnp.int32)
        .at[targets]
        .set(jnp.ones_like(cell_numbers), mode="drop")
    )
    return (columns, sea_cells, slot_cell, filled)


def local(
    spectrum, wind_speed, wind_dir, freq_kernel, dir_kernel, depth, current, land_mask, tile_owner
):
    owner_count = lax.axis_size("comp") * lax.axis_size("sub")
    group_size = -(-K // owner_count)
    padded_count = group_size * owner_count
    strip_width, strip_height = land_mask.shape
    columns, sea_cells, slot_cell, filled = layout_maps(land_mask, tile_owner[0], owner_count)
    rim_width = 2
    cell_stack = jnp.stack([depth, current[0], current[1], land_mask.astype(jnp.float32)])
    fields = padded(cell_stack.astype(jnp.bfloat16), (("tile", 1),), rim_width).astype(
        cell_stack.dtype
    )
    source = source_terms(spectrum[0, 0], wind_speed[0, 0], wind_dir[0, 0], freq_kernel, dir_kernel)
    outgoing = jnp.pad(source, ((0, padded_count - K), (0, 0)))
    arrived = lax.all_to_all(outgoing, ("comp", "sub"), split_axis=0, concat_axis=1, tiled=True)
    gathered = jnp.take(arrived, columns, axis=1, mode="clip")
    density = jnp.where(sea_cells[None, :] == 1, gathered.astype(jnp.float32), 0.0).reshape(
        group_size, strip_width, strip_height
    )
    group_index = lax.axis_index("comp") * lax.axis_size("sub") + lax.axis_index("sub")
    component = group_index * group_size + jnp.arange(group_size)
    frequency = frequencies(NF)[jnp.minimum(component // ND, NF - 1)]
    comp_angle = directions(ND)[component % ND]
    metric = row_metric(strip_height)
    group_vel = group_speed(frequency[:, None, None], fields[0][None])
    along_x = (
        (group_vel * jnp.cos(comp_angle)[:, None, None] + fields[1][None])
        * TIME_STEP
        / (CELL_SIZE * metric[None, None, :])
    )
    along_y = (
        (group_vel * jnp.sin(comp_angle)[:, None, None] + fields[2][None]) * TIME_STEP / CELL_SIZE
    )
    sea_field = fields[3][None]
    total_width = strip_width + 2 * rim_width
    inner_y = window(along_y, 2, total_width - 2, 1)
    inner_sea = window(sea_field, 2, total_width - 2, 1)
    for substep in range(NSUB):
        extended = padded(density, (("tile", 1),), 2)
        density = upwind_sweep(extended, along_x, sea_field, 1)
        density = column_sweep(density, inner_y, inner_sea)
    leaving = density.astype(jnp.bfloat16).reshape(group_size, strip_width * strip_height)
    picked = jnp.take(leaving, slot_cell, axis=1, mode="clip")
    picked = jnp.where(filled[None, :] == 1, picked, jnp.zeros((), jnp.bfloat16))
    returned = lax.all_to_all(picked, ("comp", "sub"), split_axis=1, concat_axis=0, tiled=True)
    return returned[:K].reshape(1, 1, K, PCAP)


OWNERS = 8
STRIPS = 2
GROUP = OWNERS * STRIPS
RANKS = 4
ROWS = 80
EXTRA = 16
CAP = ROWS + EXTRA
LAST = GROUP - 1
PARTS = ((0, 32), (32, 32), (64, 16))
FINAL = len(PARTS) - 1
MOST_ROWS = max(PARTS[FINAL][1] + EXTRA, *(rows for _, rows in PARTS))
WIDE = 32
TALL = 128
FIELD_ROWS = 72


def butterfly(values, pieces):
    for bit in range(3):
        step = 1 << bit
        odd = (pieces & step) != 0
        values = [jnp.where(odd, values[(j + step) % 8], values[j]) for j in range(8)]
    return values


def turn(values, by):
    by %= values.shape[0]
    if by == 0:
        return values
    return jnp.concatenate([values[-by:], values[:-by]], axis=0)


def first_sweep(d, face, bend):
    ahead = turn(d, -1)
    slope = ahead - d
    second = slope - turn(slope, 1)
    upstream = jnp.where(face > 0.0, second, turn(second, -1))
    flux = face * (0.5 * (d + ahead) - 0.5 * face * slope - bend * upstream)
    return d - (flux - turn(flux, 1))


def second_sweep(d, face, bend, lane):
    shape = d.shape
    flat = lambda v: v.reshape(shape[0] * shape[1], shape[2])
    d, face, bend = flat(d), flat(face), flat(bend)
    ahead = jnp.where(lane == TALL - 1, 0.0, pltpu.roll(d, TALL - 1, 1))
    slope = ahead - d
    second = slope - jnp.where(lane == 0, d, pltpu.roll(slope, 1, 1))
    upstream = jnp.where(face > 0.0, second, pltpu.roll(second, TALL - 1, 1))
    flux = face * (0.5 * (d + ahead) - 0.5 * face * slope - bend * upstream)
    return (d - (flux - pltpu.roll(flux, 1, 1))).reshape(shape)


def exchange_kernel(
    source_ref, depth_ref, current_ref, mask_ref, owner_ref, out_ref, place_ref,
    packed, arrived, fields, density, leaving, first_rate, second_rate, drift, tile_map,
    field_ref, angle_ref,
    go_send, go_recv, go_extra_send, go_extra_recv,
    back_send, back_recv, back_extra_send, back_extra_recv, field_send, field_recv,
):
    comp, tile, sub = lax.axis_index("comp"), lax.axis_index("tile"), lax.axis_index("sub")
    me = tile * OWNERS + comp * 2 + sub

    def partner(dc, dt, ds):
        c, t, s = lax.rem(comp + dc, 4), lax.rem(tile + dt, 2), lax.rem(sub + ds, 2)
        return t * OWNERS + c * 2 + s, {"comp": c, "tile": t, "sub": s}

    turns = [(dc, dt, ds) for dc in (2, 1, 3, 0) for dt in (0, 1) for ds in (0, 1)]
    turns = [item for item in turns if item != (0, 0, 0)]
    partners = [partner(*item) for item in turns]
    final_device = {"comp": 3, "tile": 1, "sub": 1}

    barrier = pltpu.get_barrier_semaphore()
    for _, where in partners:
        pl.semaphore_signal(barrier, inc=1, device_id=where, device_id_type=pl.DeviceIdType.MESH)

    def remote(src, dst, send, recv, where):
        return pltpu.make_async_remote_copy(
            src_ref=src, dst_ref=dst, send_sem=send, recv_sem=recv,
            device_id=where, device_id_type=pl.DeviceIdType.MESH,
        )

    def iota(shape, dim):
        return lax.broadcasted_iota(jnp.int32, shape, dim)

    def number(condition):
        return jnp.where(condition, 1.0, 0.0)

    tiles = 2 * TALL // TS
    owners = owner_ref[...].astype(jnp.float32)
    owner_rows = jnp.broadcast_to(owners, (tiles, tiles))
    eye = iota((tiles, tiles), 0) == iota((tiles, tiles), 1)
    owner_column = jnp.sum(jnp.where(eye, owner_rows, 0.0), axis=1, keepdims=True)
    earlier = (owner_column == owner_rows) & (iota((tiles, tiles), 0) < iota((tiles, tiles), 1))
    rank = jnp.sum(number(earlier), axis=0, keepdims=True)
    column = iota((tiles, 256), 1)
    spread_tile = number(lax.shift_right_logical(column, 3) == iota((tiles, 256), 0))
    target = jnp.dot(owners * 32.0 + rank * 8.0, spread_tile, preferred_element_type=jnp.float32)
    target = target + (iota((1, 256), 1) & 7).astype(jnp.float32)
    field_ref[pl.ds(0, 16), :] = depth_ref[...]
    field_ref[pl.ds(16, 16), :] = current_ref[0]
    field_ref[pl.ds(32, 16), :] = current_ref[1]
    field_ref[pl.ds(48, 16), :] = mask_ref[...].astype(jnp.float32)
    field_ref[pl.ds(64, 1), :] = target[:, :TALL]
    field_ref[pl.ds(65, 1), :] = target[:, TALL:]
    field_ref[pl.ds(66, 6), :] = jnp.zeros((6, TALL), jnp.float32)
    beside = partner(0, 1, 0)[1]
    field_copy = remote(field_ref, fields.at[tile], field_send, field_recv, beside)

    mine_owner = comp * 2 + sub
    wanted = (owner_column == mine_owner.astype(jnp.float32))
    rank_column = jnp.sum(jnp.where(eye, jnp.broadcast_to(rank, (tiles, tiles)), 0.0), axis=1, keepdims=True)
    lane_rank = lax.shift_right_logical(iota((1, 256), 1), 3) & 3
    held = wanted & (rank_column == lane_rank.astype(jnp.float32))
    tile_of = jnp.sum(jnp.where(held, iota((tiles, 256), 0).astype(jnp.float32), 0.0), axis=0, keepdims=True)
    tile_of = tile_of.astype(jnp.int32)

    def cell_x(at):
        return (lax.shift_right_logical(at, 5) - mine_owner) & 7

    def order(at):
        return (lax.shift_right_logical(at, 3) & 3) * 64 + cell_x(at) * 8 + (at & 7)

    lanes = iota((1, 256), 1)
    column_y = (tile_of & 15) * 8 + (lanes & 7)
    column_x = lax.shift_right_logical(tile_of, 4) * 8 + cell_x(lanes)
    pick = number(iota((TALL, 256), 0) == column_y)
    by_x = jnp.dot(mask_ref[...].astype(jnp.float32), pick, preferred_element_type=jnp.float32)
    mine = jnp.sum(jnp.where(iota((16, 256), 0) == column_x, by_x, 0.0), axis=0, keepdims=True)
    before = number(order(iota((256, 256), 0)) < order(iota((256, 256), 1)))
    slot = jnp.dot(jnp.broadcast_to(mine, (8, 256)), before, preferred_element_type=jnp.float32)[:1]
    slot = jnp.where(mine > 0.5, slot, -1.0).astype(jnp.int32)
    place_ref[...] = number(iota((256, 256), 0) == slot).astype(jnp.bfloat16)

    packed[...] = jnp.dot(
        source_ref[...], place_ref[...], preferred_element_type=jnp.float32
    ).astype(jnp.bfloat16)

    pl.semaphore_wait(barrier, GROUP - 1)
    field_copy.start()

    def aligned(value):
        return pl.multiple_of(value, 16)

    def go(part, number, where):
        at, rows = PARTS[part]
        return remote(
            packed.at[pl.ds(aligned(number * ROWS + at), rows)],
            arrived.at[me, pl.ds(at, rows)],
            go_send.at[part, number], go_recv.at[part, me], where,
        )

    def go_landed(part, number, where):
        at, rows = PARTS[part]
        spot = arrived.at[number, pl.ds(at, rows)]
        return remote(spot, spot, go_send.at[part, number], go_recv.at[part, number], where)

    def go_extra():
        return remote(
            packed.at[pl.ds(GROUP * ROWS, EXTRA)], arrived.at[me, pl.ds(ROWS, EXTRA)],
            go_extra_send, go_extra_recv.at[me], final_device,
        )

    for part in range(len(PARTS)):
        for number, where in partners:
            go(part, number, where).start()

    @pl.when(me != LAST)
    def _():
        go_extra().start()

    arrived[me, pl.ds(0, ROWS)] = packed[pl.ds(aligned(me * ROWS), ROWS), :]

    @pl.when(me == LAST)
    def _():
        arrived[LAST, pl.ds(ROWS, EXTRA)] = packed[pl.ds(GROUP * ROWS, EXTRA), :]

    @pl.when(me != LAST)
    def _():
        for number in range(GROUP):
            arrived[number, pl.ds(ROWS, EXTRA)] = jnp.zeros((EXTRA, 256), jnp.bfloat16)

    fields[tile] = field_ref[...]
    field_copy.wait()

    lane = lax.broadcasted_iota(jnp.int32, (1, TALL), 1)
    row_number = lax.broadcasted_iota(jnp.int32, (256, TALL), 0)
    for strip in range(STRIPS):
        for half in range(2):
            target = fields[strip, pl.ds(64 + half, 1), :].astype(jnp.int32)
            tile_map[strip, :, pl.ds(half * TALL, TALL)] = jnp.where(
                row_number == target, 1.0, 0.0
            ).astype(jnp.bfloat16)

    def whole(at):
        return jnp.concatenate([fields[strip, pl.ds(at, 16), :] for strip in range(STRIPS)], axis=0)

    depth, along_u, along_v, sea = whole(0), whole(16), whole(32), whole(48)
    above = lambda v: jnp.concatenate([v[1:], v[:1]], axis=0)
    beyond = lambda v: jnp.where(lane == TALL - 1, 0.0, pltpu.roll(v, TALL - 1, 1))
    latitude = LAT_EDGE * (2.0 * (lane.astype(jnp.float32) + 0.5) / TALL - 1.0)
    step_x = TIME_STEP / (CELL_SIZE * jnp.cos(latitude))
    half_x = 0.5 * step_x * sea * above(sea)
    half_y = 0.5 * (TIME_STEP / CELL_SIZE) * sea * beyond(sea)

    def spread(ref, at, value):
        for x in range(WIDE):
            ref[at, x] = jnp.broadcast_to(value[x : x + 1, :], (8, TALL))

    spread(drift, 0, half_x * (along_u + above(along_u)))
    spread(drift, 1, half_y * (along_v + beyond(along_v)))
    base = me * ROWS
    first_index = base // ND
    component = base + iota((CAP, TALL), 0)
    direction = component - ND * lax.shift_right_logical(component * 1821, 16)
    angle = (2.0 * math.pi / ND) * (direction.astype(jnp.float32) + 0.5)
    angle_ref[0] = jnp.cos(angle)
    angle_ref[1] = jnp.sin(angle)
    for which in range(4):
        index = jnp.minimum(first_index + which, NF - 1).astype(jnp.float32)
        exponent = jnp.broadcast_to(index * math.log(FREQ_RATIO), (1, TALL))
        frequency = FREQ_BASE * jnp.exp(exponent)
        angular = 2.0 * math.pi * frequency
        deep_number = angular * angular / GRAVITY
        wavenumber = deep_number / jnp.sqrt(jnp.tanh(deep_number * depth))
        relative = jnp.minimum(wavenumber * depth, KH_LIMIT)
        sinh = 0.5 * (jnp.exp(2.0 * relative) - jnp.exp(-2.0 * relative))
        speed = (0.5 + relative / sinh) * angular / wavenumber
        spread(first_rate, which, half_x * (speed + above(speed)))
        spread(second_rate, which, half_y * (speed + beyond(speed)))

    pieces = lax.shift_right_logical(lax.broadcasted_iota(jnp.int32, (1, 256), 1), 5)
    row8 = lax.broadcasted_iota(jnp.int32, (8, TALL), 0)
    wide_lane = lax.broadcasted_iota(jnp.int32, (WIDE * 8, TALL), 1)

    def back(part, number, where):
        at, rows = PARTS[part]
        return remote(
            leaving.at[number, pl.ds(at, rows)],
            out_ref.at[pl.ds(aligned(me * ROWS + at), rows)],
            back_send.at[part, number], back_recv.at[part, me], where,
        )

    def back_landed(part, number, where):
        at, rows = PARTS[part]
        spot = out_ref.at[pl.ds(aligned(number * ROWS + at), rows)]
        return remote(spot, spot, back_send.at[part, number], back_recv.at[part, number], where)

    def back_extra(number, where):
        return remote(
            leaving.at[number, pl.ds(ROWS, EXTRA)], out_ref.at[pl.ds(GROUP * ROWS, EXTRA)],
            back_extra_send.at[number], back_extra_recv, where,
        )

    for part in range(len(PARTS)):
        at, rows = PARTS[part]
        height = rows + EXTRA if part == FINAL else rows
        for number, where in partners:
            go_landed(part, number, where).wait_recv()
        if part == FINAL:

            @pl.when(me == LAST)
            def _():
                for number, where in partners:
                    spot = arrived.at[number, pl.ds(ROWS, EXTRA)]
                    remote(spot, spot, go_extra_send, go_extra_recv.at[number], where).wait_recv()

        for strip in range(STRIPS):
            blocks = [
                arrived[strip * OWNERS + o, pl.ds(at, height), :].astype(jnp.float32)
                for o in range(OWNERS)
            ]
            blocks = butterfly(blocks, pieces)
            lined = []
            for xx in range(TS):
                block = blocks[-xx % 8]
                if xx:
                    block = pltpu.roll(block, 256 - 32 * xx, 1)
                lined.append(block.astype(jnp.bfloat16))
            placed = jnp.dot(
                jnp.concatenate(lined, axis=0), tile_map[strip], preferred_element_type=jnp.float32
            )
            for xx in range(TS):
                for half in range(2):
                    density[strip * 16 + half * TS + xx, pl.ds(0, height)] = placed[
                        xx * height : (xx + 1) * height, half * TALL : (half + 1) * TALL
                    ]

        def chunk(step, carry):
            start = base + at + step * 8
            index = start // ND
            table = index - first_index
            later = jnp.minimum(table + 1, 3)
            new = row8 >= (index + 1) * ND - start
            here = pl.ds(pl.multiple_of(step * 8, 8), 8)
            angle_at = pl.ds(pl.multiple_of(at + step * 8, 8), 8)
            cos, sin = angle_ref[0, angle_at, :], angle_ref[1, angle_at, :]
            face_x = jnp.where(new[None], first_rate[later], first_rate[table]) * cos[None] + drift[0]
            face_y = jnp.where(new[None], second_rate[later], second_rate[table]) * sin[None] + drift[1]
            bend_x = (1.0 - face_x * face_x) * (1.0 / 6.0)
            bend_y = (1.0 - face_y * face_y) * (1.0 / 6.0)
            d = density[:, here, :]
            for substep in range(NSUB):
                d = first_sweep(d, face_x, bend_x)
                d = second_sweep(d, face_y, bend_y, wide_lane)
            density[:, here, :] = d
            return carry

        count = rows // 8 if part < FINAL else jnp.where(me == LAST, height // 8, rows // 8)
        lax.fori_loop(0, count, chunk, 0)

        for strip in range(STRIPS):
            lined = [
                jnp.concatenate(
                    [density[strip * 16 + half * TS + xx, pl.ds(0, height)] for half in range(2)], axis=1
                ).astype(jnp.bfloat16)
                for xx in range(TS)
            ]
            sorted_rows = lax.dot_general(
                jnp.concatenate(lined, axis=0), tile_map[strip], (((1,), (1,)), ((), ())),
                preferred_element_type=jnp.float32,
            )
            blocks = []
            for xx in range(TS):
                block = sorted_rows[xx * height : (xx + 1) * height]
                blocks.append(pltpu.roll(block, 32 * xx, 1) if xx else block)
            blocks = butterfly(blocks, pieces)
            for o in range(OWNERS):
                leaving[strip * OWNERS + o, pl.ds(at, height)] = blocks[-o % 8].astype(jnp.bfloat16)

        for number, where in partners:
            back(part, number, where).start()
        if part == FINAL:

            @pl.when(me == LAST)
            def _():
                for number, where in partners:
                    back_extra(number, where).start()

    out_ref[pl.ds(aligned(me * ROWS), ROWS), :] = leaving[me, pl.ds(0, ROWS), :]

    @pl.when(me == LAST)
    def _():
        out_ref[pl.ds(GROUP * ROWS, EXTRA), :] = leaving[LAST, pl.ds(ROWS, EXTRA), :]

    for part in range(len(PARTS)):
        for number, where in partners:
            go(part, number, where).wait_send()
            back(part, number, where).wait_send()
            back_landed(part, number, where).wait_recv()

    @pl.when(me != LAST)
    def _():
        go_extra().wait_send()
        spot = out_ref.at[pl.ds(GROUP * ROWS, EXTRA)]
        remote(spot, spot, back_extra_send.at[LAST], back_extra_recv, final_device).wait_recv()

    @pl.when(me == LAST)
    def _():
        for number, where in partners:
            back_extra(number, where).wait_send()


def exchange(source, depth, current, land_mask, tile_owner):
    dma = pltpu.SemaphoreType.DMA
    vmem = pl.BlockSpec(memory_space=pltpu.VMEM)
    return pl.pallas_call(
        exchange_kernel,
        out_shape=[
            jax.ShapeDtypeStruct((K, 256), jnp.bfloat16),
            jax.ShapeDtypeStruct((256, 256), jnp.bfloat16),
        ],
        in_specs=[vmem] * 5,
        out_specs=[vmem] * 2,
        scratch_shapes=[
            pltpu.VMEM((K, 256), jnp.bfloat16),
            pltpu.VMEM((GROUP, CAP, 256), jnp.bfloat16),
            pltpu.VMEM((STRIPS, FIELD_ROWS, TALL), jnp.float32),
            pltpu.VMEM((WIDE, MOST_ROWS, TALL), jnp.float32),
            pltpu.VMEM((GROUP, CAP, 256), jnp.bfloat16),
            pltpu.VMEM((4, WIDE, 8, TALL), jnp.float32),
            pltpu.VMEM((4, WIDE, 8, TALL), jnp.float32),
            pltpu.VMEM((2, WIDE, 8, TALL), jnp.float32),
            pltpu.VMEM((STRIPS, 256, 256), jnp.bfloat16),
            pltpu.VMEM((FIELD_ROWS, TALL), jnp.float32),
            pltpu.VMEM((2, CAP, TALL), jnp.float32),
            dma((len(PARTS), GROUP)), dma((len(PARTS), GROUP)), dma, dma((GROUP,)),
            dma((len(PARTS), GROUP)), dma((len(PARTS), GROUP)), dma((GROUP,)), dma, dma, dma,
        ],
        compiler_params=pltpu.CompilerParams(
            collective_id=0, has_side_effects=True, vmem_limit_bytes=40 * 1024 * 1024
        ),
    )(source, depth, current, land_mask, tile_owner)


def grouped(
    spectrum, wind_speed, wind_dir, freq_kernel, dir_kernel, depth, current, land_mask, tile_owner
):
    source = source_terms(spectrum[0, 0], wind_speed[0, 0], wind_dir[0, 0], freq_kernel, dir_kernel)
    returned, place = exchange(source, depth, current, land_mask, tile_owner)
    result = lax.dot_general(
        returned, place, (((1,), (1,)), ((), ())), preferred_element_type=jnp.float32
    ).astype(jnp.bfloat16)
    return result.reshape(1, 1, K, PCAP)


def solution(mesh):
    sizes = mesh.shape
    fits = (sizes["comp"], sizes["sub"], sizes["tile"]) == (4, 2, STRIPS)
    placed = (
        P(("ens", "tile"), ("comp", "sub"), None, None),
        P(("ens", "tile"), ("comp", "sub"), None),
        P(("ens", "tile"), ("comp", "sub"), None),
        P(),
        P(),
        P("tile", None),
        P(None, "tile", None),
        P("tile", None),
        P("tile", None),
    )
    return jax.shard_map(
        grouped if fits else local,
        mesh=mesh,
        in_specs=placed,
        out_specs=P(("ens", "tile"), ("comp", "sub"), None, None),
        check_vma=False,
    )
```

```python
import math

import jax
import jax.numpy as jnp
from jax import lax
from jax.experimental import pallas as pl
from jax.experimental.pallas import tpu as pltpu
from jax.sharding import PartitionSpec as P

NF = 36
ND = 36
TS = 8
NSUB = 2
K = 1296
PCAP = 256


GRAVITY = 9.81
FREQ_BASE = 0.035
FREQ_RATIO = 1.1
TIME_STEP = 450.0
CELL_SIZE = 27750.0
LAT_EDGE = 64.0 * math.pi / 180.0
WIND_RATE = 0.1
BREAK_RATE = 0.15
ENERGY_REF = 1.5
TRANSFER_RATE = 0.2
KH_LIMIT = 10.0


def padded(value, sides, width):
    for axis, dim in sides:
        devices, length = (lax.axis_size(axis), value.shape[dim])
        up = [(i, (i + 1) % devices) for i in range(devices)]
        down = [(j, i) for i, j in up]
        last = lax.slice_in_dim(value, length - width, length, axis=dim)
        leading = lax.slice_in_dim(value, 0, width, axis=dim)
        before = lax.ppermute(last, axis, up)
        after = lax.ppermute(leading, axis, down)
        value = jnp.concatenate([before, value, after], axis=dim)
    return value


def frequencies(how_many):
    return FREQ_BASE * jnp.power(jnp.float32(FREQ_RATIO), jnp.arange(how_many).astype(jnp.float32))


def directions(how_many):
    return 2.0 * math.pi * (jnp.arange(how_many).astype(jnp.float32) + 0.5) / how_many


def row_metric(rows_total):
    latitude = LAT_EDGE * (
        2.0 * (jnp.arange(rows_total).astype(jnp.float32) + 0.5) / rows_total - 1.0
    )
    return jnp.cos(latitude)


def group_speed(frequency, sea_depth):
    angular = 2.0 * math.pi * frequency
    deep_number = angular * angular / GRAVITY
    wavenumber = deep_number / jnp.sqrt(jnp.tanh(deep_number * sea_depth))
    relative = jnp.minimum(wavenumber * sea_depth, KH_LIMIT)
    group_ratio = 0.5 + relative / jnp.sinh(2.0 * relative)
    return group_ratio * angular / wavenumber


def heading_parts(heading):
    quarter = 0.25 * heading
    square = quarter * quarter
    sine = 1.0 / 5040.0 - square / 362880.0
    sine = quarter * (1.0 - square * (1.0 / 6.0 - square * (1.0 / 120.0 - square * sine)))
    cosine = 1.0 / 720.0 - square * (1.0 / 40320.0 - square / 3628800.0)
    cosine = 1.0 - square * (0.5 - square * (1.0 / 24.0 - square * cosine))
    for _ in range(2):
        sine, cosine = 2.0 * sine * cosine, 1.0 - 2.0 * sine * sine
    return cosine, sine


def source_terms(spectrum_block, wind_speed, heading, freq_kernel, dir_kernel):
    freq_count = freq_kernel.shape[0]
    dir_count = dir_kernel.shape[0]
    points = spectrum_block.shape[1]
    energy = spectrum_block.astype(jnp.float32).reshape(freq_count, dir_count, points)
    frequency = frequencies(freq_count)
    angles = directions(dir_count)
    weighted = jnp.sum(energy, axis=1) * frequency[:, None]
    first_moment = jnp.sum(weighted, axis=0)
    total = FREQ_BASE * sum(FREQ_RATIO**i for i in range(freq_count))
    mean_energy = first_moment / (dir_count * total)
    mean_freq = jnp.sum(weighted * frequency[:, None], axis=0) / first_moment
    phase_speed = GRAVITY / (2.0 * math.pi * frequency)
    heading_cos, heading_sin = heading_parts(heading)
    forcing = (
        wind_speed[None, None, :]
        / phase_speed[:, None, None]
        * (
            jnp.cos(angles)[None, :, None] * heading_cos[None, None, :]
            + jnp.sin(angles)[None, :, None] * heading_sin[None, None, :]
        )
        - 1.0
    )
    growth = WIND_RATE * jnp.maximum(forcing, 0.0)
    damping = (
        BREAK_RATE
        * (frequency[:, None, None] / mean_freq[None, None, :])
        * jnp.square(mean_energy / ENERGY_REF)[None, None, :]
    )
    coupled = jnp.einsum("ab,bjp->ajp", freq_kernel, energy, precision=lax.Precision.HIGH)
    coupled = jnp.einsum("cj,ajp->acp", dir_kernel, coupled, precision=lax.Precision.HIGH)
    transfer = TRANSFER_RATE * energy * coupled / mean_energy[None, None, :]
    updated = (energy + growth * energy + transfer) / (1.0 + damping)
    return updated.reshape(freq_count * dir_count, points).astype(jnp.bfloat16)


def window(values, begin_at, end_at, along):
    return lax.slice_in_dim(values, begin_at, end_at, axis=along)


def upwind_sweep(density, courant, sea_mask, along):
    length = density.shape[along]
    behind = window(density, 0, length - 3, along)
    centre = window(density, 1, length - 2, along)
    ahead_one = window(density, 2, length - 1, along)
    beyond = window(density, 3, length, along)
    face_courant = 0.5 * (
        window(courant, 1, length - 2, along) + window(courant, 2, length - 1, along)
    )
    face_courant = (
        face_courant
        * window(sea_mask, 1, length - 2, along)
        * window(sea_mask, 2, length - 1, along)
    )
    curvature = (1.0 - face_courant * face_courant) / 6.0
    middle = 0.5 * (centre + ahead_one) - 0.5 * face_courant * (ahead_one - centre)
    upstream = jnp.where(
        face_courant > 0.0, ahead_one - 2.0 * centre + behind, beyond - 2.0 * ahead_one + centre
    )
    face_flux = face_courant * (middle - curvature * upstream)
    return window(density, 2, length - 2, along) - (
        window(face_flux, 1, length - 3, along) - window(face_flux, 0, length - 4, along)
    )


def column_sweep(density, courant, sea_mask):
    widths = ((0, 0), (0, 0), (2, 2))
    return upwind_sweep(
        jnp.pad(density, widths), jnp.pad(courant, widths), jnp.pad(sea_mask, widths), 2
    )


def layout_maps(mask_strip, owners, owner_count):
    strip_width, strip_height = mask_strip.shape
    tiles_across = strip_width // TS
    tiles_down = strip_height // TS
    tile_cells = (
        mask_strip.reshape(tiles_across, TS, tiles_down, TS)
        .transpose(0, 2, 1, 3)
        .reshape(tiles_across * tiles_down, TS * TS)
    )
    counts = jnp.sum(tile_cells, axis=1)
    tile_index = jnp.arange(tiles_across * tiles_down)
    earlier = (owners[None, :] == owners[:, None]) & (tile_index[None, :] < tile_index[:, None])
    offsets = jnp.sum(jnp.where(earlier, counts[None, :], 0), axis=1)
    rank_within = jnp.cumsum(tile_cells, axis=1) - tile_cells
    columns = owners[:, None] * PCAP + offsets[:, None] + rank_within
    columns = (
        columns.reshape(tiles_across, tiles_down, TS, TS)
        .transpose(0, 2, 1, 3)
        .reshape(strip_width * strip_height)
    )
    sea_cells = mask_strip.reshape(strip_width * strip_height)
    targets = jnp.where(sea_cells == 1, columns, owner_count * PCAP)
    cell_numbers = jnp.arange(strip_width * strip_height)
    slot_cell = (
        jnp.zeros((owner_count * PCAP,), jnp.int32).at[targets].set(cell_numbers, mode="drop")
    )
    filled = (
        jnp.zeros((owner_count * PCAP,), jnp.int32)
        .at[targets]
        .set(jnp.ones_like(cell_numbers), mode="drop")
    )
    return (columns, sea_cells, slot_cell, filled)


def local(
    spectrum, wind_speed, wind_dir, freq_kernel, dir_kernel, depth, current, land_mask, tile_owner
):
    owner_count = lax.axis_size("comp") * lax.axis_size("sub")
    group_size = -(-K // owner_count)
    padded_count = group_size * owner_count
    strip_width, strip_height = land_mask.shape
    columns, sea_cells, slot_cell, filled = layout_maps(land_mask, tile_owner[0], owner_count)
    rim_width = 2
    cell_stack = jnp.stack([depth, current[0], current[1], land_mask.astype(jnp.float32)])
    fields = padded(cell_stack.astype(jnp.bfloat16), (("tile", 1),), rim_width).astype(
        cell_stack.dtype
    )
    source = source_terms(spectrum[0, 0], wind_speed[0, 0], wind_dir[0, 0], freq_kernel, dir_kernel)
    outgoing = jnp.pad(source, ((0, padded_count - K), (0, 0)))
    arrived = lax.all_to_all(outgoing, ("comp", "sub"), split_axis=0, concat_axis=1, tiled=True)
    gathered = jnp.take(arrived, columns, axis=1, mode="clip")
    density = jnp.where(sea_cells[None, :] == 1, gathered.astype(jnp.float32), 0.0).reshape(
        group_size, strip_width, strip_height
    )
    group_index = lax.axis_index("comp") * lax.axis_size("sub") + lax.axis_index("sub")
    component = group_index * group_size + jnp.arange(group_size)
    frequency = frequencies(NF)[jnp.minimum(component // ND, NF - 1)]
    comp_angle = directions(ND)[component % ND]
    metric = row_metric(strip_height)
    group_vel = group_speed(frequency[:, None, None], fields[0][None])
    along_x = (
        (group_vel * jnp.cos(comp_angle)[:, None, None] + fields[1][None])
        * TIME_STEP
        / (CELL_SIZE * metric[None, None, :])
    )
    along_y = (
        (group_vel * jnp.sin(comp_angle)[:, None, None] + fields[2][None]) * TIME_STEP / CELL_SIZE
    )
    sea_field = fields[3][None]
    total_width = strip_width + 2 * rim_width
    inner_y = window(along_y, 2, total_width - 2, 1)
    inner_sea = window(sea_field, 2, total_width - 2, 1)
    for substep in range(NSUB):
        extended = padded(density, (("tile", 1),), 2)
        density = upwind_sweep(extended, along_x, sea_field, 1)
        density = column_sweep(density, inner_y, inner_sea)
    leaving = density.astype(jnp.bfloat16).reshape(group_size, strip_width * strip_height)
    picked = jnp.take(leaving, slot_cell, axis=1, mode="clip")
    picked = jnp.where(filled[None, :] == 1, picked, jnp.zeros((), jnp.bfloat16))
    returned = lax.all_to_all(picked, ("comp", "sub"), split_axis=1, concat_axis=0, tiled=True)
    return returned[:K].reshape(1, 1, K, PCAP)


OWNERS = 8
STRIPS = 2
GROUP = OWNERS * STRIPS
RANKS = 4
ROWS = 80
EXTRA = 16
CAP = ROWS + EXTRA
LAST = GROUP - 1
PARTS = ((0, 32), (32, 32), (64, 16))
FINAL = len(PARTS) - 1
MOST_ROWS = max(PARTS[FINAL][1] + EXTRA, *(rows for _, rows in PARTS))
WIDE = 32
TALL = 128
FIELD_ROWS = 72


def butterfly(values, pieces):
    for bit in range(3):
        step = 1 << bit
        odd = (pieces & step) != 0
        values = [jnp.where(odd, values[(j + step) % 8], values[j]) for j in range(8)]
    return values


def turn(values, by):
    by %= values.shape[0]
    if by == 0:
        return values
    return jnp.concatenate([values[-by:], values[:-by]], axis=0)


def first_sweep(d, face, bend):
    ahead = turn(d, -1)
    slope = ahead - d
    second = slope - turn(slope, 1)
    upstream = jnp.where(face > 0.0, second, turn(second, -1))
    flux = face * (0.5 * (d + ahead) - 0.5 * face * slope - bend * upstream)
    return d - (flux - turn(flux, 1))


def second_sweep(d, face, bend, lane):
    shape = d.shape
    flat = lambda v: v.reshape(shape[0] * shape[1], shape[2])
    d, face, bend = flat(d), flat(face), flat(bend)
    ahead = jnp.where(lane == TALL - 1, 0.0, pltpu.roll(d, TALL - 1, 1))
    slope = ahead - d
    second = slope - jnp.where(lane == 0, d, pltpu.roll(slope, 1, 1))
    upstream = jnp.where(face > 0.0, second, pltpu.roll(second, TALL - 1, 1))
    flux = face * (0.5 * (d + ahead) - 0.5 * face * slope - bend * upstream)
    return (d - (flux - pltpu.roll(flux, 1, 1))).reshape(shape)


def exchange_kernel(
    source_ref, depth_ref, current_ref, mask_ref, owner_ref, out_ref, place_ref,
    packed, arrived, fields, density, leaving, first_rate, second_rate, drift, tile_map,
    field_ref, angle_ref,
    go_send, go_recv, go_extra_send, go_extra_recv,
    back_send, back_recv, back_extra_send, back_extra_recv, field_send, field_recv,
):
    comp, tile, sub = lax.axis_index("comp"), lax.axis_index("tile"), lax.axis_index("sub")
    me = tile * OWNERS + comp * 2 + sub

    def partner(dc, dt, ds):
        c, t, s = lax.rem(comp + dc, 4), lax.rem(tile + dt, 2), lax.rem(sub + ds, 2)
        return t * OWNERS + c * 2 + s, {"comp": c, "tile": t, "sub": s}

    turns = [(dc, dt, ds) for dc in (2, 1, 3, 0) for dt in (0, 1) for ds in (0, 1)]
    turns = [item for item in turns if item != (0, 0, 0)]
    partners = [partner(*item) for item in turns]
    final_device = {"comp": 3, "tile": 1, "sub": 1}

    barrier = pltpu.get_barrier_semaphore()
    for _, where in partners:
        pl.semaphore_signal(barrier, inc=1, device_id=where, device_id_type=pl.DeviceIdType.MESH)

    def remote(src, dst, send, recv, where):
        return pltpu.make_async_remote_copy(
            src_ref=src, dst_ref=dst, send_sem=send, recv_sem=recv,
            device_id=where, device_id_type=pl.DeviceIdType.MESH,
        )

    def iota(shape, dim):
        return lax.broadcasted_iota(jnp.int32, shape, dim)

    def number(condition):
        return jnp.where(condition, 1.0, 0.0)

    tiles = 2 * TALL // TS
    owners = owner_ref[...].astype(jnp.float32)
    owner_rows = jnp.broadcast_to(owners, (tiles, tiles))
    eye = iota((tiles, tiles), 0) == iota((tiles, tiles), 1)
    owner_column = jnp.sum(jnp.where(eye, owner_rows, 0.0), axis=1, keepdims=True)
    earlier = (owner_column == owner_rows) & (iota((tiles, tiles), 0) < iota((tiles, tiles), 1))
    rank = jnp.sum(number(earlier), axis=0, keepdims=True)
    column = iota((tiles, 256), 1)
    spread_tile = number(lax.shift_right_logical(column, 3) == iota((tiles, 256), 0))
    target = jnp.dot(owners * 32.0 + rank * 8.0, spread_tile, preferred_element_type=jnp.float32)
    target = target + (iota((1, 256), 1) & 7).astype(jnp.float32)
    field_ref[pl.ds(0, 16), :] = depth_ref[...]
    field_ref[pl.ds(16, 16), :] = current_ref[0]
    field_ref[pl.ds(32, 16), :] = current_ref[1]
    field_ref[pl.ds(48, 16), :] = mask_ref[...].astype(jnp.float32)
    field_ref[pl.ds(64, 1), :] = target[:, :TALL]
    field_ref[pl.ds(65, 1), :] = target[:, TALL:]
    field_ref[pl.ds(66, 6), :] = jnp.zeros((6, TALL), jnp.float32)
    beside = partner(0, 1, 0)[1]
    field_copy = remote(field_ref, fields.at[tile], field_send, field_recv, beside)

    mine_owner = comp * 2 + sub
    wanted = (owner_column == mine_owner.astype(jnp.float32))
    rank_column = jnp.sum(jnp.where(eye, jnp.broadcast_to(rank, (tiles, tiles)), 0.0), axis=1, keepdims=True)
    lane_rank = lax.shift_right_logical(iota((1, 256), 1), 3) & 3
    held = wanted & (rank_column == lane_rank.astype(jnp.float32))
    tile_of = jnp.sum(jnp.where(held, iota((tiles, 256), 0).astype(jnp.float32), 0.0), axis=0, keepdims=True)
    tile_of = tile_of.astype(jnp.int32)

    def cell_x(at):
        return (lax.shift_right_logical(at, 5) - mine_owner) & 7

    def order(at):
        return (lax.shift_right_logical(at, 3) & 3) * 64 + cell_x(at) * 8 + (at & 7)

    lanes = iota((1, 256), 1)
    column_y = (tile_of & 15) * 8 + (lanes & 7)
    column_x = lax.shift_right_logical(tile_of, 4) * 8 + cell_x(lanes)
    pick = number(iota((TALL, 256), 0) == column_y)
    by_x = jnp.dot(mask_ref[...].astype(jnp.float32), pick, preferred_element_type=jnp.float32)
    mine = jnp.sum(jnp.where(iota((16, 256), 0) == column_x, by_x, 0.0), axis=0, keepdims=True)
    before = number(order(iota((256, 256), 0)) < order(iota((256, 256), 1)))
    slot = jnp.dot(jnp.broadcast_to(mine, (8, 256)), before, preferred_element_type=jnp.float32)[:1]
    slot = jnp.where(mine > 0.5, slot, -1.0).astype(jnp.int32)
    place_ref[...] = number(iota((256, 256), 0) == slot).astype(jnp.bfloat16)

    def pack(part):
        at, rows = PARTS[part]
        spans = [(group * ROWS + at, rows) for group in range(GROUP)]
        if part == FINAL:
            spans.append((GROUP * ROWS, EXTRA))
        block = jnp.concatenate([source_ref[pl.ds(*span), :] for span in spans], axis=0)
        block = jnp.dot(block, place_ref[...], preferred_element_type=jnp.float32)
        block = block.astype(jnp.bfloat16)
        done = 0
        for start, size in spans:
            packed[pl.ds(start, size), :] = block[done : done + size]
            done += size

    pack(0)

    pl.semaphore_wait(barrier, GROUP - 1)
    field_copy.start()

    def aligned(value):
        return pl.multiple_of(value, 16)

    def go(part, number, where):
        at, rows = PARTS[part]
        return remote(
            packed.at[pl.ds(aligned(number * ROWS + at), rows)],
            arrived.at[me, pl.ds(at, rows)],
            go_send.at[part, number], go_recv.at[part, me], where,
        )

    def go_landed(part, number, where):
        at, rows = PARTS[part]
        spot = arrived.at[number, pl.ds(at, rows)]
        return remote(spot, spot, go_send.at[part, number], go_recv.at[part, number], where)

    def go_extra():
        return remote(
            packed.at[pl.ds(GROUP * ROWS, EXTRA)], arrived.at[me, pl.ds(ROWS, EXTRA)],
            go_extra_send, go_extra_recv.at[me], final_device,
        )

    for part in range(len(PARTS)):
        if part:
            pack(part)
        for number, where in partners:
            go(part, number, where).start()

    @pl.when(me != LAST)
    def _():
        go_extra().start()

    arrived[me, pl.ds(0, ROWS)] = packed[pl.ds(aligned(me * ROWS), ROWS), :]

    @pl.when(me == LAST)
    def _():
        arrived[LAST, pl.ds(ROWS, EXTRA)] = packed[pl.ds(GROUP * ROWS, EXTRA), :]

    @pl.when(me != LAST)
    def _():
        for number in range(GROUP):
            arrived[number, pl.ds(ROWS, EXTRA)] = jnp.zeros((EXTRA, 256), jnp.bfloat16)

    fields[tile] = field_ref[...]
    field_copy.wait()

    lane = lax.broadcasted_iota(jnp.int32, (1, TALL), 1)
    row_number = lax.broadcasted_iota(jnp.int32, (256, TALL), 0)
    for strip in range(STRIPS):
        for half in range(2):
            target = fields[strip, pl.ds(64 + half, 1), :].astype(jnp.int32)
            tile_map[strip, :, pl.ds(half * TALL, TALL)] = jnp.where(
                row_number == target, 1.0, 0.0
            ).astype(jnp.bfloat16)

    def whole(at):
        return jnp.concatenate([fields[strip, pl.ds(at, 16), :] for strip in range(STRIPS)], axis=0)

    depth, along_u, along_v, sea = whole(0), whole(16), whole(32), whole(48)
    above = lambda v: jnp.concatenate([v[1:], v[:1]], axis=0)
    beyond = lambda v: jnp.where(lane == TALL - 1, 0.0, pltpu.roll(v, TALL - 1, 1))
    latitude = LAT_EDGE * (2.0 * (lane.astype(jnp.float32) + 0.5) / TALL - 1.0)
    step_x = TIME_STEP / (CELL_SIZE * jnp.cos(latitude))
    half_x = 0.5 * step_x * sea * above(sea)
    half_y = 0.5 * (TIME_STEP / CELL_SIZE) * sea * beyond(sea)

    def spread(ref, at, value):
        for x in range(WIDE):
            ref[at, x] = jnp.broadcast_to(value[x : x + 1, :], (8, TALL))

    spread(drift, 0, half_x * (along_u + above(along_u)))
    spread(drift, 1, half_y * (along_v + beyond(along_v)))
    base = me * ROWS
    first_index = base // ND
    component = base + iota((CAP, TALL), 0)
    direction = component - ND * lax.shift_right_logical(component * 1821, 16)
    angle = (2.0 * math.pi / ND) * (direction.astype(jnp.float32) + 0.5)
    angle_ref[0] = jnp.cos(angle)
    angle_ref[1] = jnp.sin(angle)
    for which in range(4):
        index = jnp.minimum(first_index + which, NF - 1).astype(jnp.float32)
        exponent = jnp.broadcast_to(index * math.log(FREQ_RATIO), (1, TALL))
        frequency = FREQ_BASE * jnp.exp(exponent)
        angular = 2.0 * math.pi * frequency
        deep_number = angular * angular / GRAVITY
        wavenumber = deep_number / jnp.sqrt(jnp.tanh(deep_number * depth))
        relative = jnp.minimum(wavenumber * depth, KH_LIMIT)
        sinh = 0.5 * (jnp.exp(2.0 * relative) - jnp.exp(-2.0 * relative))
        speed = (0.5 + relative / sinh) * angular / wavenumber
        spread(first_rate, which, half_x * (speed + above(speed)))
        spread(second_rate, which, half_y * (speed + beyond(speed)))

    pieces = lax.shift_right_logical(lax.broadcasted_iota(jnp.int32, (1, 256), 1), 5)
    row8 = lax.broadcasted_iota(jnp.int32, (8, TALL), 0)
    wide_lane = lax.broadcasted_iota(jnp.int32, (WIDE * 8, TALL), 1)

    def back(part, number, where):
        at, rows = PARTS[part]
        return remote(
            leaving.at[number, pl.ds(at, rows)],
            out_ref.at[pl.ds(aligned(me * ROWS + at), rows)],
            back_send.at[part, number], back_recv.at[part, me], where,
        )

    def back_landed(part, number, where):
        at, rows = PARTS[part]
        spot = out_ref.at[pl.ds(aligned(number * ROWS + at), rows)]
        return remote(spot, spot, back_send.at[part, number], back_recv.at[part, number], where)

    def back_extra(number, where):
        return remote(
            leaving.at[number, pl.ds(ROWS, EXTRA)], out_ref.at[pl.ds(GROUP * ROWS, EXTRA)],
            back_extra_send.at[number], back_extra_recv, where,
        )

    for part in range(len(PARTS)):
        at, rows = PARTS[part]
        height = rows + EXTRA if part == FINAL else rows
        for number, where in partners:
            go_landed(part, number, where).wait_recv()
        if part == FINAL:

            @pl.when(me == LAST)
            def _():
                for number, where in partners:
                    spot = arrived.at[number, pl.ds(ROWS, EXTRA)]
                    remote(spot, spot, go_extra_send, go_extra_recv.at[number], where).wait_recv()

        for strip in range(STRIPS):
            blocks = [
                arrived[strip * OWNERS + o, pl.ds(at, height), :].astype(jnp.float32)
                for o in range(OWNERS)
            ]
            blocks = butterfly(blocks, pieces)
            lined = []
            for xx in range(TS):
                block = blocks[-xx % 8]
                if xx:
                    block = pltpu.roll(block, 256 - 32 * xx, 1)
                lined.append(block.astype(jnp.bfloat16))
            placed = jnp.dot(
                jnp.concatenate(lined, axis=0), tile_map[strip], preferred_element_type=jnp.float32
            )
            for xx in range(TS):
                for half in range(2):
                    density[strip * 16 + half * TS + xx, pl.ds(0, height)] = placed[
                        xx * height : (xx + 1) * height, half * TALL : (half + 1) * TALL
                    ]

        def chunk(step, carry):
            start = base + at + step * 8
            index = start // ND
            table = index - first_index
            later = jnp.minimum(table + 1, 3)
            new = row8 >= (index + 1) * ND - start
            here = pl.ds(pl.multiple_of(step * 8, 8), 8)
            angle_at = pl.ds(pl.multiple_of(at + step * 8, 8), 8)
            cos, sin = angle_ref[0, angle_at, :], angle_ref[1, angle_at, :]
            face_x = jnp.where(new[None], first_rate[later], first_rate[table]) * cos[None] + drift[0]
            face_y = jnp.where(new[None], second_rate[later], second_rate[table]) * sin[None] + drift[1]
            bend_x = (1.0 - face_x * face_x) * (1.0 / 6.0)
            bend_y = (1.0 - face_y * face_y) * (1.0 / 6.0)
            d = density[:, here, :]
            for substep in range(NSUB):
                d = first_sweep(d, face_x, bend_x)
                d = second_sweep(d, face_y, bend_y, wide_lane)
            density[:, here, :] = d
            return carry

        count = rows // 8 if part < FINAL else jnp.where(me == LAST, height // 8, rows // 8)
        lax.fori_loop(0, count, chunk, 0)

        for strip in range(STRIPS):
            lined = [
                jnp.concatenate(
                    [density[strip * 16 + half * TS + xx, pl.ds(0, height)] for half in range(2)], axis=1
                ).astype(jnp.bfloat16)
                for xx in range(TS)
            ]
            sorted_rows = lax.dot_general(
                jnp.concatenate(lined, axis=0), tile_map[strip], (((1,), (1,)), ((), ())),
                preferred_element_type=jnp.float32,
            )
            blocks = []
            for xx in range(TS):
                block = sorted_rows[xx * height : (xx + 1) * height]
                blocks.append(pltpu.roll(block, 32 * xx, 1) if xx else block)
            blocks = butterfly(blocks, pieces)
            for o in range(OWNERS):
                leaving[strip * OWNERS + o, pl.ds(at, height)] = blocks[-o % 8].astype(jnp.bfloat16)

        for number, where in partners:
            back(part, number, where).start()
        if part == FINAL:

            @pl.when(me == LAST)
            def _():
                for number, where in partners:
                    back_extra(number, where).start()

    out_ref[pl.ds(aligned(me * ROWS), ROWS), :] = leaving[me, pl.ds(0, ROWS), :]

    @pl.when(me == LAST)
    def _():
        out_ref[pl.ds(GROUP * ROWS, EXTRA), :] = leaving[LAST, pl.ds(ROWS, EXTRA), :]

    for part in range(len(PARTS)):
        for number, where in partners:
            go(part, number, where).wait_send()
            back(part, number, where).wait_send()
            back_landed(part, number, where).wait_recv()

    @pl.when(me != LAST)
    def _():
        go_extra().wait_send()
        spot = out_ref.at[pl.ds(GROUP * ROWS, EXTRA)]
        remote(spot, spot, back_extra_send.at[LAST], back_extra_recv, final_device).wait_recv()

    @pl.when(me == LAST)
    def _():
        for number, where in partners:
            back_extra(number, where).wait_send()


def exchange(source, depth, current, land_mask, tile_owner):
    dma = pltpu.SemaphoreType.DMA
    vmem = pl.BlockSpec(memory_space=pltpu.VMEM)
    return pl.pallas_call(
        exchange_kernel,
        out_shape=[
            jax.ShapeDtypeStruct((K, 256), jnp.bfloat16),
            jax.ShapeDtypeStruct((256, 256), jnp.bfloat16),
        ],
        in_specs=[vmem] * 5,
        out_specs=[vmem] * 2,
        scratch_shapes=[
            pltpu.VMEM((K, 256), jnp.bfloat16),
            pltpu.VMEM((GROUP, CAP, 256), jnp.bfloat16),
            pltpu.VMEM((STRIPS, FIELD_ROWS, TALL), jnp.float32),
            pltpu.VMEM((WIDE, MOST_ROWS, TALL), jnp.float32),
            pltpu.VMEM((GROUP, CAP, 256), jnp.bfloat16),
            pltpu.VMEM((4, WIDE, 8, TALL), jnp.float32),
            pltpu.VMEM((4, WIDE, 8, TALL), jnp.float32),
            pltpu.VMEM((2, WIDE, 8, TALL), jnp.float32),
            pltpu.VMEM((STRIPS, 256, 256), jnp.bfloat16),
            pltpu.VMEM((FIELD_ROWS, TALL), jnp.float32),
            pltpu.VMEM((2, CAP, TALL), jnp.float32),
            dma((len(PARTS), GROUP)), dma((len(PARTS), GROUP)), dma, dma((GROUP,)),
            dma((len(PARTS), GROUP)), dma((len(PARTS), GROUP)), dma((GROUP,)), dma, dma, dma,
        ],
        compiler_params=pltpu.CompilerParams(
            collective_id=0, has_side_effects=True, vmem_limit_bytes=40 * 1024 * 1024
        ),
    )(source, depth, current, land_mask, tile_owner)


def grouped(
    spectrum, wind_speed, wind_dir, freq_kernel, dir_kernel, depth, current, land_mask, tile_owner
):
    source = source_terms(spectrum[0, 0], wind_speed[0, 0], wind_dir[0, 0], freq_kernel, dir_kernel)
    returned, place = exchange(source, depth, current, land_mask, tile_owner)
    result = lax.dot_general(
        returned, place, (((1,), (1,)), ((), ())), preferred_element_type=jnp.float32
    ).astype(jnp.bfloat16)
    return result.reshape(1, 1, K, PCAP)


def solution(mesh):
    sizes = mesh.shape
    fits = (sizes["comp"], sizes["sub"], sizes["tile"]) == (4, 2, STRIPS)
    placed = (
        P(("ens", "tile"), ("comp", "sub"), None, None),
        P(("ens", "tile"), ("comp", "sub"), None),
        P(("ens", "tile"), ("comp", "sub"), None),
        P(),
        P(),
        P("tile", None),
        P(None, "tile", None),
        P("tile", None),
        P("tile", None),
    )
    return jax.shard_map(
        grouped if fits else local,
        mesh=mesh,
        in_specs=placed,
        out_specs=P(("ens", "tile"), ("comp", "sub"), None, None),
        check_vma=False,
    )
```
